128 devices in a mesh: rep: 4 (over z_lo, core), fsdp: 32 (over z_hi, x, y).
Axes of the slice: x: 4, y: 4, z: 4 (z_hi: 2, z_lo: 2; z = z_hi * 2 + z_lo), core: 2. Of those that a mesh axis runs over, the one named last changes fastest.
Arguments:
- tokens: bfloat16 [8192, 8192], P('fsdp'), as said below
- query_ckpt: float32 [4, 8192, 1024], P('rep', 'fsdp'), as said below
- key_value_ckpt: float32 [4, 8192, 256], P('rep', 'fsdp'), as said below
- numerators: int32 [4], replicated, may hold values from 1 to 8
Outputs:
- context: bfloat16 [8192, 1024], P('fsdp')
The draws below stay inside these ranges and needn't reach their ends.
Inputs may be any that keep to these rules, and one draw needn't show every extreme that they name: `tokens`: hidden states of mixed scales. `query_ckpt`: checkpoint weights. `key_value_ckpt`: checkpoint weights.
All inputs are finite; a program needn't handle non-finite values.
Results may differ from the reference program's by a relative error of at most 0.0081.
Values may be sent and summed in bfloat16 or wider, within the bound.
No kernel may reach another device: no remote copies, remote signals or barrier semaphores. Data moves between devices by JAX's collectives and lax.ppermute only.
A program may use at most 128 MiB of HBM per device.

```python
import math
import jax
import jax.numpy as jnp
from jax import lax

D = 8192
HEAD = 128
TOKENS = 8192
LENGTH = 8192
QW = 1024
KW = 128
N_REP = 4


def common_basis(key):
    basis_key = jax.random.fold_in(key, 77)
    return jax.random.normal(basis_key, (D, HEAD), jnp.float32) / math.sqrt(D)


def draw_query_ckpt(key, part):
    key = jax.random.fold_in(key, 1)
    base_key, noise_key = jax.random.split(key, 2)
    base_part = jax.random.normal(base_key, (D, QW), jnp.float32) * (0.5 / math.sqrt(D))
    noise_part = jax.random.normal(noise_key, (N_REP, D, QW), jnp.float32) * (0.5 / math.sqrt(D))
    return base_part[None] + noise_part


def draw_key_value_ckpt(key, part):
    key_basis = common_basis(key)
    key = jax.random.fold_in(key, 2)
    first_key, second_key, third_key = jax.random.split(key, 3)
    key_noise = jax.random.normal(first_key, (N_REP, D, KW), jnp.float32) * (0.6 / math.sqrt(D))
    value_base = jax.random.normal(second_key, (D, KW), jnp.float32) * (0.7 / math.sqrt(D))
    value_noise = jax.random.normal(third_key, (N_REP, D, KW), jnp.float32) * (0.7 / math.sqrt(D))
    key_part = key_basis[None] + key_noise
    value_part = value_base[None] + value_noise
    return jnp.concatenate([key_part, value_part], axis=2)


def draw_tokens(key, part):
    key = jax.random.fold_in(key, 3)
    first_key, second_key, third_key = jax.random.split(key, 3)
    raw_draw = jax.random.normal(first_key, (TOKENS, D), jnp.float32)
    row_scale = jnp.exp(jax.random.uniform(second_key, (TOKENS, 1), jnp.float32, math.log(0.3), math.log(3.0)))
    col_scale = jnp.exp(jax.random.uniform(third_key, (1, D), jnp.float32, math.log(0.3), math.log(3.0)))
    return (raw_draw * row_scale * col_scale).astype(jnp.bfloat16)


def set_ends(values, rng, smallest, high):
    place = [jax.random.randint(jax.random.fold_in(rng, axis), (), 0, length) for axis, length in enumerate(values.shape)]
    widest = values.shape.index(max(values.shape))
    neighbour = place[:widest] + [(place[widest] + 1) % values.shape[widest]] + place[widest + 1:]
    return values.at[tuple(place)].set(smallest).at[tuple(neighbour)].set(high)


def setup_inputs(seed: int = 0) -> dict:
    key_of = jax.random.split(jax.random.key(seed), 5)
    tokens = draw_tokens(jax.random.fold_in(key_of[4], 71), 0)
    query_ckpt = draw_query_ckpt(jax.random.fold_in(key_of[4], 71), 0)
    key_value_ckpt = draw_key_value_ckpt(jax.random.fold_in(key_of[4], 71), 0)
    numerators = set_ends(jax.random.randint(key_of[3], (N_REP,), 1, 9), jax.random.fold_in(key_of[3], 1), 1, 8).astype(jnp.int32)
    return {"tokens": tokens, "query_ckpt": query_ckpt, "key_value_ckpt": key_value_ckpt, "numerators": numerators}


theta_base = 500000.0
eps_norm = 1e-05
masked_score = -1e+30

def averaged(checkpoints, numerators):
    weight_sum = jnp.sum(numerators).astype(jnp.float32)
    shares = numerators.astype(jnp.float32) / weight_sum
    return lax.optimization_barrier(jnp.sum(shares[:, None, None] * checkpoints, axis=0)).astype(jnp.bfloat16)

def rms_normed(hidden):
    wide_copy = hidden.astype(jnp.float32)
    return (wide_copy * lax.rsqrt(lax.optimization_barrier(jnp.mean(wide_copy * wide_copy, axis=-1, keepdims=True)) + eps_norm)).astype(jnp.bfloat16)

def rotary(values, positions):
    half_size = values.shape[-1] // 2
    inverse_freq = jnp.exp(-(jnp.arange(half_size, dtype=jnp.float32) * (2.0 / values.shape[-1])) * math.log(theta_base))
    angles = positions.astype(jnp.float32)[:, None] * inverse_freq[None, :]
    cosine_table = jnp.cos(angles)[:, None, :]
    sine_table = jnp.sin(angles)[:, None, :]
    first_half = values[..., :half_size]
    second_half = values[..., half_size:]
    return jnp.concatenate([first_half * cosine_table - second_half * sine_table, second_half * cosine_table + first_half * sine_table], axis=-1)

def attend_heads(queries, pair_rows, query_pos, key_pos):
    head_size = queries.shape[-1]
    key_rows = pair_rows[:, :head_size]
    value_rows = pair_rows[:, head_size:]
    score_scale = 1.0 / math.sqrt(head_size)
    allowed = key_pos[None, :] <= query_pos[:, None]

    def one_head(query_head):
        scores = jnp.dot(query_head, key_rows.T, preferred_element_type=jnp.float32) * score_scale
        scores = jnp.where(allowed, scores, masked_score)
        row_top = lax.optimization_barrier(jnp.max(scores, axis=1, keepdims=True))
        weights_exp = jnp.exp(scores - row_top)
        norm_sum = lax.optimization_barrier(jnp.sum(weights_exp, axis=1, keepdims=True))
        mixed_out = jnp.dot(weights_exp.astype(jnp.bfloat16), value_rows, preferred_element_type=jnp.float32) / norm_sum
        return mixed_out.astype(jnp.bfloat16)
    head_outs = lax.map(one_head, jnp.transpose(queries, (1, 0, 2)))
    return jnp.transpose(head_outs, (1, 0, 2)).reshape(queries.shape[0], -1)

def project(normed, query_avg, pair_avg, positions):
    queries = jnp.dot(normed, query_avg, preferred_element_type=jnp.float32)
    pair_proj = jnp.dot(normed, pair_avg, preferred_element_type=jnp.float32)
    row_count = normed.shape[0]
    query_rot = rotary(queries.reshape(row_count, queries.shape[1] // HEAD, HEAD), positions).astype(jnp.bfloat16)
    key_rot = rotary(pair_proj[:, None, :HEAD], positions)[:, 0, :].astype(jnp.bfloat16)
    pair_rows = jnp.concatenate([key_rot, pair_proj[:, HEAD:].astype(jnp.bfloat16)], axis=1)
    return (query_rot, pair_rows)

def reference(tokens, query_ckpt, key_value_ckpt, numerators):
    query_avg = averaged(query_ckpt, numerators)
    pair_avg = averaged(key_value_ckpt, numerators)
    sequences = tokens.reshape(TOKENS // LENGTH, LENGTH, D)
    positions = jnp.arange(LENGTH, dtype=jnp.int32)

    def one_sequence(seq_tokens):
        normed = rms_normed(seq_tokens)
        query_rot, pair_rows = project(normed, query_avg, pair_avg, positions)
        return attend_heads(query_rot, pair_rows, positions, positions)
    outputs = lax.map(one_sequence, sequences)
    return outputs.reshape(TOKENS, -1)
```

```python
import functools
import math

import jax
import jax.numpy as jnp
import numpy as np
from jax import lax
from jax.experimental import pallas as pl
from jax.experimental.pallas import tpu as pltpu
from jax.sharding import Mesh, PartitionSpec as P

theta_base = 500000.0
eps_norm = 1e-05
masked_score = -1e30
HEAD = 128
F32 = jnp.float32
BF16 = jnp.bfloat16
VMEM = pltpu.VMEM
SMEM = pltpu.SMEM
NT = (((1,), (1,)), ((), ()))
SWAP = [(0, 1), (1, 0)]


def params(mib=56):
    return pltpu.CompilerParams(vmem_limit_bytes=mib * 1024 * 1024)


def cost(flops, nbytes, trans=0):
    return pl.CostEstimate(flops=flops, bytes_accessed=nbytes, transcendentals=trans)


def vspec():
    return pl.BlockSpec(memory_space=VMEM)


def sspec():
    return pl.BlockSpec(memory_space=SMEM)


def pair_order():
    order = []
    for r in range(4):
        order += list(range(16 * r, 16 * r + 16))
        order += list(range(64 + 16 * r, 64 + 16 * r + 16))
        order += list(range(128 + 32 * r, 128 + 32 * r + 32))
    return order


def norm_kernel(idx, x_ref, own_ref, send_ref):
    zh, c = idx[0], idx[1]
    x = x_ref[...].astype(F32)
    scale = lax.rsqrt(jnp.mean(x * x, axis=-1, keepdims=True) + eps_norm)
    half = own_ref.shape[1]
    quarter = send_ref.shape[1]
    own = x_ref[:, pl.ds(pl.multiple_of(zh * half, half), half)].astype(F32)
    own_ref[...] = (own * scale).astype(BF16)
    start = pl.multiple_of((1 - zh) * half + c * quarter, quarter)
    send = x_ref[:, pl.ds(start, quarter)].astype(F32)
    send_ref[...] = (send * scale).astype(BF16)


def normalise(idx, tokens):
    rows, width = tokens.shape
    step = 32
    return pl.pallas_call(
        norm_kernel,
        grid=(rows // step,),
        in_specs=[sspec(), pl.BlockSpec((step, width), lambda i: (i, 0))],
        out_specs=[
            pl.BlockSpec((step, width // 2), lambda i: (i, 0)),
            pl.BlockSpec((step, width // 4), lambda i: (i, 0)),
        ],
        out_shape=[
            jax.ShapeDtypeStruct((rows, width // 2), BF16),
            jax.ShapeDtypeStruct((rows, width // 4), BF16),
        ],
        compiler_params=params(),
        cost_estimate=cost(rows * width * 4, rows * width * 4),
        name="normalise",
    )(idx, tokens)


def prep_kernel(idx, share, q_ref, kv_ref, perm_ref, send_ref, keep_ref):
    c = idx[1]
    s = share[0]
    kvt = lax.dot_general(
        perm_ref[...], kv_ref[...] * s, NT, precision=lax.Precision.HIGHEST,
        preferred_element_type=F32,
    )
    for zl in range(2):
        for cc in range(2):
            col = (zl * 2 + cc) * 256
            row = (zl * 2 + cc) * 64

            @pl.when(cc == c)
            def _():
                keep_ref[zl, 0:256] = q_ref[:, col:col + 256] * s
                keep_ref[zl, 256:320] = kvt[row:row + 64]

            @pl.when(cc != c)
            def _():
                send_ref[zl, 0:256] = q_ref[:, col:col + 256] * s
                send_ref[zl, 256:320] = kvt[row:row + 64]


def prepare(idx, share, q, kv, perm):
    shape = jax.ShapeDtypeStruct((2, 320, 256), F32)
    return pl.pallas_call(
        prep_kernel,
        in_specs=[sspec(), sspec(), vspec(), vspec(), vspec()],
        out_specs=[vspec(), vspec()],
        out_shape=[shape, shape],
        compiler_params=params(),
        cost_estimate=cost(256 * 256 * 256 * 12, 3 << 20),
        name="prepare",
    )(idx, share, q, kv, perm)


def kv_kernel(w_ref, *refs):
    xs, out_ref = refs[:-1], refs[-1]
    blocks = w_ref.shape[0]
    per = blocks // len(xs)
    acc = jnp.zeros(out_ref.shape, F32)
    for i, x_ref in enumerate(xs):
        for j in range(per):
            acc += lax.dot_general(
                w_ref[i * per + j], x_ref[:, j * 256:(j + 1) * 256], NT,
                preferred_element_type=F32,
            )
    out_ref[...] = acc.astype(out_ref.dtype)


def q_kernel(w_ref, *refs):
    xs, out_ref = refs[:-1], refs[-1]
    blocks = w_ref.shape[0]
    per = blocks // len(xs)
    acc = jnp.zeros(out_ref.shape, F32)
    for i, x_ref in enumerate(xs):
        for j in range(per):
            acc += jnp.dot(
                x_ref[:, j * 256:(j + 1) * 256], w_ref[i * per + j],
                preferred_element_type=F32,
            )
    out_ref[...] = acc.astype(out_ref.dtype)


def project(kernel, w, xs, shape, dtype, name):
    return pl.pallas_call(
        kernel,
        in_specs=[vspec()] * (1 + len(xs)),
        out_specs=vspec(),
        out_shape=jax.ShapeDtypeStruct(shape, dtype),
        compiler_params=params(),
        cost_estimate=cost(2 * shape[0] * shape[1] * 4096, 4 << 20),
        name=name,
    )(w, *xs)


def kv_finish_kernel(own_ref, got_ref, cos_ref, sin_ref, out_ref):
    t = own_ref[...] + got_ref[...]
    u, w = t[0:16], t[16:32]
    cos, sin = cos_ref[...], sin_ref[...]
    lo = (u * cos - w * sin).astype(BF16)
    hi = (w * cos + u * sin).astype(BF16)
    v = t[32:64].astype(BF16)
    for h in range(2):
        cols = slice(h * 128, (h + 1) * 128)
        out_ref[h, 0:16] = lo[:, cols]
        out_ref[h, 16:32] = hi[:, cols]
        out_ref[h, 32:64] = v[:, cols]


def q_finish_kernel(own_ref, got_ref, cos_ref, sin_ref, out_ref):
    t = own_ref[...] + got_ref[...].astype(F32)
    cos, sin = cos_ref[...], sin_ref[...]
    for h in range(2):
        u = t[:, h * 128:h * 128 + 64]
        w = t[:, h * 128 + 64:h * 128 + 128]
        out_ref[h] = jnp.concatenate([u * cos - w * sin, w * cos + u * sin], axis=1).astype(BF16)


def finish(kernel, args, shape, name):
    return pl.pallas_call(
        kernel,
        in_specs=[vspec()] * len(args),
        out_specs=vspec(),
        out_shape=jax.ShapeDtypeStruct(shape, BF16),
        compiler_params=params(),
        cost_estimate=cost(1 << 18, 1 << 19),
        name=name,
    )(*args)


CHUNK = 4
EXP_SCALE = math.log2(math.e) / math.sqrt(HEAD)


def attend_kernel(idx, qa_ref, qb_ref, kv_ref, oa_ref, ob_ref):
    f, c = idx[2], idx[1]
    last = f // CHUNK

    def load(j):
        kt, vt = [], []
        for b in range(CHUNK):
            blk = kv_ref.at[j * CHUNK + b]
            kt.append(jnp.concatenate(
                [blk[r, 0:16] for r in range(4)] + [blk[r, 16:32] for r in range(4)], axis=0))
            vt.append(jnp.concatenate([blk[r, 32:64] for r in range(4)], axis=0))
        return jnp.concatenate(kt, axis=1), jnp.concatenate(vt, axis=1)

    def step(q, j, carry, masked):
        m, l, acc = carry
        kt, vt = load(j)
        s = jnp.dot(q, kt, preferred_element_type=F32)
        if masked:
            row = lax.broadcasted_iota(jnp.int32, s.shape, 0) + f * 256
            col = lax.broadcasted_iota(jnp.int32, s.shape, 1)
            pos = (j * CHUNK + col // 128) * 256 + c * 128 + col % 128
            s = jnp.where(pos <= row, s, masked_score)
        top = jnp.maximum(m, jnp.max(s, axis=1, keepdims=True))
        p = jnp.exp2((s - top) * EXP_SCALE)
        fix = jnp.exp2((m - top) * EXP_SCALE)
        psum = p[:, 0:128]
        for b in range(1, CHUNK):
            psum = psum + p[:, b * 128:(b + 1) * 128]
        l = l * fix + psum
        acc = acc * fix + lax.dot_general(p.astype(BF16), vt, NT, preferred_element_type=F32)
        return top, l, acc

    for q_ref, o_ref in ((qa_ref, oa_ref), (qb_ref, ob_ref)):
        for h in range(2):
            q = q_ref[h]
            carry = (
                jnp.full((256, 1), masked_score, F32),
                jnp.zeros((256, 128), F32),
                jnp.zeros((256, 128), F32),
            )
            carry = lax.fori_loop(0, last, lambda j, s: step(q, j, s, False), carry)
            m, l, acc = step(q, last, carry, True)
            o_ref[0, h * 256:(h + 1) * 256] = acc
            o_ref[1, h * 256:(h + 1) * 256] = jnp.broadcast_to(m, (256, 128))
            o_ref[2, h * 256:(h + 1) * 256] = l


def attend(idx, qa, qb, kv):
    shape = jax.ShapeDtypeStruct((3, 512, 128), F32)
    return pl.pallas_call(
        attend_kernel,
        in_specs=[sspec(), vspec(), vspec(), vspec()],
        out_specs=[vspec(), vspec()],
        out_shape=[shape, shape],
        compiler_params=params(),
        cost_estimate=cost(4 * 1024 * 4096 * 128, 4 << 20, 1024 * 4096),
        name="attend",
    )(idx, qa, qb, kv)


def combine_kernel(a_ref, b_ref, out_ref):
    ma, mb = a_ref[1], b_ref[1]
    top = jnp.maximum(ma, mb)
    fa = jnp.exp2((ma - top) * EXP_SCALE)
    fb = jnp.exp2((mb - top) * EXP_SCALE)
    total = jnp.sum(a_ref[2] * fa + b_ref[2] * fb, axis=1, keepdims=True)
    o = ((a_ref[0] * fa + b_ref[0] * fb) / total).astype(BF16)
    for h in range(2):
        out_ref[:, h * 128:(h + 1) * 128] = o[h * 256:(h + 1) * 256]


def combine(a, b):
    return pl.pallas_call(
        combine_kernel,
        in_specs=[vspec(), vspec()],
        out_specs=vspec(),
        out_shape=jax.ShapeDtypeStruct((256, 256), BF16),
        compiler_params=params(),
        cost_estimate=cost(1 << 19, 2 << 20),
        name="combine",
    )(a, b)


def local(tokens, query_ckpt, key_value_ckpt, numerators):
    zl, c, zh = lax.axis_index("zl"), lax.axis_index("c"), lax.axis_index("zh")
    f = lax.axis_index(("zh", "x", "y"))
    r = zl * 2 + c
    idx = jnp.stack([zh, c, f]).astype(jnp.int32)
    share = (numerators[r].astype(F32) / jnp.sum(numerators).astype(F32)).reshape(1)

    perm = np.zeros((256, 256), np.float32)
    perm[np.arange(256), pair_order()] = 1.0
    send, keep = prepare(idx, share, query_ckpt[0], key_value_ckpt[0], jnp.asarray(perm))
    half = keep + lax.ppermute(send, "c", SWAP)
    mine = jnp.where(zl == 0, half[0], half[1])
    theirs = jnp.where(zl == 0, half[1], half[0]).astype(BF16)
    w = (mine + lax.ppermute(theirs, "zl", SWAP).astype(F32)).astype(BF16)
    wq, wkv = w[0:256], w[256:320]

    own, out = normalise(idx, tokens)
    got = lax.ppermute(out, "zh", SWAP)
    other = lax.ppermute(got, "c", SWAP)
    first = jnp.where(c == 0, got, other)
    second = jnp.where(c == 0, other, got)

    plane = ("x", "y")
    wkv_all = lax.all_to_all(jnp.broadcast_to(wkv[None], (16, 64, 256)), plane, 0, 0)
    wq_all = lax.all_to_all(jnp.broadcast_to(wq[None], (16, 256, 256)), plane, 0, 0)

    inverse_freq = jnp.exp(
        -(jnp.arange(64, dtype=F32) * (2.0 / HEAD)) * math.log(theta_base)
    )
    positions = (f * 256 + jnp.arange(256, dtype=jnp.int32)).astype(F32)
    angles = positions[:, None] * inverse_freq[None, :]
    cos, sin = jnp.cos(angles), jnp.sin(angles)
    my_freq = lax.dynamic_slice_in_dim(inverse_freq, r * 16, 16)
    angles_t = positions[None, :] * my_freq[:, None]
    cos_t, sin_t = jnp.cos(angles_t), jnp.sin(angles_t)

    kv_theirs = project(kv_kernel, wkv_all, (first, second), (64, 256), F32, "kv_theirs")
    kv_got = lax.ppermute(kv_theirs, "zh", SWAP)
    kv_own = project(kv_kernel, wkv_all, (own,), (64, 256), F32, "kv_own")
    pair = finish(kv_finish_kernel, (kv_own, kv_got, cos_t, sin_t), (2, 64, 128), "kv_finish")
    kv_all = lax.all_to_all(
        jnp.broadcast_to(pair[None], (64, 2, 64, 128)).reshape(128, 64, 128),
        ("zh", "x", "y", "zl", "c"), 0, 0,
    )

    q_theirs = project(q_kernel, wq_all, (first, second), (256, 256), BF16, "q_theirs")
    q_got = lax.ppermute(q_theirs, "zh", SWAP)
    q_own = project(q_kernel, wq_all, (own,), (256, 256), F32, "q_own")
    qa = finish(q_finish_kernel, (q_own, q_got, cos, sin), (2, 256, 128), "q_finish")
    qb = lax.ppermute(qa, "c", SWAP)

    oa, ob = attend(idx, qa, qb, kv_all.reshape(32, 4, 64, 128))
    mixed = combine(oa, lax.ppermute(ob, "c", SWAP))
    return lax.all_gather(mixed, ("zl", "c"), axis=1, tiled=True)


def solution(mesh):
    grid = Mesh(mesh.devices.reshape(2, 2, 2, 4, 4), ("zl", "c", "zh", "x", "y"))
    rep, fsdp = ("zl", "c"), ("zh", "x", "y")
    in_specs = (P(fsdp, None), P(rep, fsdp, None), P(rep, fsdp, None), P())
    return jax.shard_map(
        local, mesh=grid, in_specs=in_specs, out_specs=P(fsdp, None), check_vma=False
    )
```

```python
import functools
import math

import jax
import jax.numpy as jnp
from jax import lax
from jax.experimental import pallas as pl
from jax.experimental.pallas import tpu as pltpu
from jax.sharding import Mesh, PartitionSpec as P

theta_base = 500000.0
eps_norm = 1e-05
masked_score = -1e30
HEAD = 128
F32 = jnp.float32
BF16 = jnp.bfloat16
VMEM = pltpu.VMEM
SMEM = pltpu.SMEM
NT = (((1,), (1,)), ((), ()))
SWAP = [(0, 1), (1, 0)]


def params(mib=20):
    return pltpu.CompilerParams(vmem_limit_bytes=mib * 1024 * 1024)


def cost(flops, nbytes, trans=0):
    return pl.CostEstimate(flops=flops, bytes_accessed=nbytes, transcendentals=trans)


def vspec():
    return pl.BlockSpec(memory_space=VMEM)


def sspec():
    return pl.BlockSpec(memory_space=SMEM)


def pair_order():
    row = lax.broadcasted_iota(jnp.int32, (256, 256), 0)
    col = lax.broadcasted_iota(jnp.int32, (256, 256), 1)
    r, t = row // 64, row % 64
    key = r * 16 + t + jnp.where(t < 16, 0, 48)
    return jnp.where(col == jnp.where(t < 32, key, r * 32 + t + 96), 1.0, 0.0)


def norm_kernel(idx, x_ref, scale_ref, send_ref):
    zh, c = idx[0], idx[1]
    x = x_ref[...].astype(F32)
    scale = lax.rsqrt(jnp.mean(x * x, axis=-1, keepdims=True) + eps_norm)
    scale_ref[...] = jnp.broadcast_to(scale, scale_ref.shape)
    quarter = send_ref.shape[1]
    start = pl.multiple_of(((1 - zh) * 2 + c) * quarter, quarter)
    send_ref[...] = normed(x_ref, start, quarter, scale)


def normed(x_ref, start, width, scale):
    return (x_ref[:, pl.ds(start, width)].astype(F32) * scale).astype(BF16)


def normalise(idx, tokens):
    rows, width = tokens.shape
    step = 128
    return pl.pallas_call(
        norm_kernel,
        grid=(rows // step,),
        in_specs=[sspec(), pl.BlockSpec((step, width), lambda i: (i, 0))],
        out_specs=[
            pl.BlockSpec((step, 128), lambda i: (i, 0)),
            pl.BlockSpec((step, width // 4), lambda i: (i, 0)),
        ],
        out_shape=[
            jax.ShapeDtypeStruct((rows, 128), F32),
            jax.ShapeDtypeStruct((rows, width // 4), BF16),
        ],
        compiler_params=params(),
        cost_estimate=cost(rows * width * 4, rows * width * 3),
        name="normalise",
    )(idx, tokens)


def share_of(idx, num, shape):
    r = idx[3]
    total = num[0] + num[1] + num[2] + num[3]
    mine = jnp.full(shape, num[r], jnp.int32).astype(F32)
    return mine / jnp.full(shape, total, jnp.int32).astype(F32)


def prep_kernel(idx, num, q_ref, kv_ref, send_ref, keep_ref):
    c = idx[1]
    s = share_of(idx, num, (1, 256))
    kvt = lax.dot_general(
        pair_order(), kv_ref[0] * s, NT, precision=lax.Precision.HIGHEST,
        preferred_element_type=F32,
    )
    for zl in range(2):
        keep = pl.multiple_of((zl * 2 + c) * 256, 256)
        send = pl.multiple_of((zl * 2 + 1 - c) * 256, 256)
        first, second = kvt[zl * 128:zl * 128 + 64], kvt[zl * 128 + 64:zl * 128 + 128]
        for ref, col, pair in (
            (keep_ref, keep, jnp.where(c == 0, first, second)),
            (send_ref, send, jnp.where(c == 0, second, first)),
        ):
            for half in range(2):
                at = half * 160
                ref[zl, at:at + 128] = q_ref[0, half * 128:half * 128 + 128, pl.ds(col, 256)] * s
                ref[zl, at + 128:at + 160] = pair[half * 32:half * 32 + 32]


def prepare(idx, num, q, kv):
    shape = jax.ShapeDtypeStruct((2, 320, 256), F32)
    return pl.pallas_call(
        prep_kernel,
        in_specs=[sspec(), sspec()] + [vspec()] * 2,
        out_specs=[vspec(), vspec()],
        out_shape=[shape, shape],
        compiler_params=params(),
        cost_estimate=cost(1 << 20, 3 << 20),
        name="prepare",
    )(idx, num, q, kv)


def ring(step):
    return [(i, (i + step) % 4) for i in range(4)]


def gather_plane(w):
    lower, upper = w[0:160], w[160:320]
    lower = jnp.stack([lower] + [lax.ppermute(lower, "y", ring(d)) for d in (1, 3, 2)])
    upper = jnp.stack([upper] + [lax.ppermute(upper, "x", ring(d)) for d in (1, 3, 2)])
    lower, upper = lax.optimization_barrier((lower, upper))
    lowers = [lower] + [lax.ppermute(lower, "x", ring(d)) for d in (1, 3, 2)]
    uppers = [upper] + [lax.ppermute(upper, "y", ring(d)) for d in (1, 3, 2)]
    return lowers + uppers


def plane_block(idx, w_refs, j):
    back = (0, 1, 3, 2)
    dx, dy = j // 4, j % 4
    low, up = w_refs[dx], w_refs[4 + dy]
    q = jnp.concatenate([low[dy, 0:128], up[dx, 0:128]], axis=0)
    pair = jnp.concatenate([low[dy, 128:160], up[dx, 128:160]], axis=0)
    return q, pair, ((idx[4] + 4 - back[dx]) % 4) * 4 + (idx[5] + 4 - back[dy]) % 4


def accumulate(idx, w_refs, block):
    acc, pair_acc = None, None
    for j in range(16):
        w, pair, at = plane_block(idx, w_refs, j)
        x = block(at)
        part = jnp.dot(x, w, preferred_element_type=F32)
        pair_part = lax.dot_general(x, pair, NT, preferred_element_type=F32)
        acc = part if acc is None else acc + part
        pair_acc = pair_part if pair_acc is None else pair_acc + pair_part
    row = lax.broadcasted_iota(jnp.int32, (64, 64), 0)
    col = lax.broadcasted_iota(jnp.int32, (64, 64), 1)
    pair_acc = lax.dot_general(
        jnp.where(row == col, 1.0, 0.0), pair_acc, NT, precision=lax.Precision.HIGHEST,
        preferred_element_type=F32,
    )
    return acc, pair_acc


def own_kernel(idx, *refs):
    w_refs, (x_ref, scale_ref, q_ref, pair_ref) = refs[:-4], refs[-4:]
    scale = scale_ref[:, 0:1]

    def block(at):
        return normed(x_ref, pl.multiple_of((idx[0] * 16 + at) * 256, 256), 256, scale)

    q_ref[...], pair_ref[...] = accumulate(idx, w_refs, block)


def theirs_kernel(idx, *refs):
    w_refs, (xa_ref, xb_ref, out_ref) = refs[:-3], refs[-3:]

    def block(at):
        cols = pl.ds(pl.multiple_of((at % 8) * 256, 256), 256)
        return jnp.where(at // 8 == idx[1], xa_ref[:, cols], xb_ref[:, cols])

    q, pair = accumulate(idx, w_refs, block)
    high = pair.astype(BF16)
    out_ref[0:256] = q.astype(BF16)
    out_ref[256:320] = high
    out_ref[320:384] = (pair - high.astype(F32)).astype(BF16)


def project(kernel, args, outs, name):
    return pl.pallas_call(
        kernel,
        in_specs=[sspec()] + [vspec()] * (len(args) - 1),
        out_specs=[vspec()] * len(outs),
        out_shape=outs,
        compiler_params=params(),
        cost_estimate=cost(2 * 256 * 320 * 4096, 5 << 20),
        name=name,
    )(*args)


def pair_finish_kernel(own_ref, got_ref, cos_ref, sin_ref, out_ref):
    t = own_ref[...] + (got_ref[256:320].astype(F32) + got_ref[320:384].astype(F32))
    u, w = t[0:16], t[16:32]
    cos, sin = cos_ref[...], sin_ref[...]
    key = jnp.concatenate([u * cos - w * sin, w * cos + u * sin], axis=0)
    val = t[32:64]
    for r in range(4):
        cols = slice(r * 64, (r + 1) * 64)
        piece = jnp.concatenate([key[:, cols], val[:, cols]], axis=1).astype(BF16)
        for f in range(out_ref.shape[0]):
            out_ref[f, r] = piece


def q_finish_kernel(own_ref, got_ref, cos_ref, sin_ref, out_ref):
    t = own_ref[...] + got_ref[0:256].astype(F32)
    cos, sin = cos_ref[...], sin_ref[...]
    for h in range(2):
        u = t[:, h * 128:h * 128 + 64]
        w = t[:, h * 128 + 64:h * 128 + 128]
        rotated = jnp.concatenate([u * cos - w * sin, w * cos + u * sin], axis=1)
        out_ref[h] = rotated.T.astype(BF16)


def finish(kernel, args, shape, name):
    return pl.pallas_call(
        kernel,
        in_specs=[vspec()] * 4,
        out_specs=vspec(),
        out_shape=jax.ShapeDtypeStruct(shape, BF16),
        compiler_params=params(),
        cost_estimate=cost(1 << 18, 1 << 20),
        name=name,
    )(*args)


CHUNK = 512
KEYS = 2048
EXP_SCALE = math.log2(math.e) / math.sqrt(HEAD)
STAT = 144


def attend_kernel(idx, *refs):
    q_refs, kv_ref = refs[0:4], refs[4]
    o_refs = refs[5:9]
    k_s, v_s, qx, s0, s1 = refs[9:]
    scores = (s0, s1)
    f, r = idx[2], idx[3]
    lane = lax.broadcasted_iota(jnp.int32, (32, 128), 1)
    col = lax.broadcasted_iota(jnp.int32, (128, 128), 1)
    row = lax.broadcasted_iota(jnp.int32, (128, 128), 0)
    for p in range(KEYS // 128):
        ks, vs = [], []
        for rr in range(4):
            a = kv_ref[2 * p, rr].astype(F32)
            b = kv_ref[2 * p + 1, rr].astype(F32)
            ks.append(jnp.where(lane < 64, a, pltpu.roll(b, 64, 1)).astype(BF16))
            vs.append(jnp.where(lane < 64, pltpu.roll(a, 64, 1), b).astype(BF16))
        key = jnp.concatenate([x[0:16] for x in ks] + [x[16:32] for x in ks], axis=0)
        k_s[p * 128:(p + 1) * 128, 0:128] = key.T
        blk = 2 * p + row // 64
        extra = jnp.where((blk == f) & (col == row % 64), 1.0, 0.0)
        extra = jnp.where((blk > f) & (col == 64), 1.0, extra)
        k_s[p * 128:(p + 1) * 128, 128:256] = extra.astype(BF16)
        v_s[:, p * 128:(p + 1) * 128] = jnp.concatenate(vs, axis=0)
    t = lax.broadcasted_iota(jnp.int32, (128, 256), 0)
    i = lax.broadcasted_iota(jnp.int32, (128, 256), 1)
    hidden = ((t < 64) & (64 * r + t > i)) | (t == 64)
    qx[...] = jnp.where(hidden, masked_score, 0.0).astype(BF16)

    def queries(h):
        return jnp.concatenate([q_refs[h // 2][h % 2], qx[...]], axis=0)

    def score(h, j, q, top):
        s = jnp.dot(k_s[j * CHUNK:(j + 1) * CHUNK], q, preferred_element_type=F32)
        scores[h % 2][j * CHUNK:(j + 1) * CHUNK] = s
        part = jnp.max(s.reshape(CHUNK // 8, 8, 256), axis=0)
        return part if top is None else jnp.maximum(top, part)

    chunks = KEYS // CHUNK
    tops, q = None, queries(0)
    for j in range(chunks):
        tops = score(0, j, q, tops)
    for h in range(8):
        top = jnp.max(tops, axis=0, keepdims=True)
        tops, acc, total = None, None, None
        if h < 7:
            q = queries(h + 1)
        for j in range(chunks):
            if h < 7:
                tops = score(h + 1, j, q, tops)
            p = jnp.exp2((scores[h % 2][j * CHUNK:(j + 1) * CHUNK] - top) * EXP_SCALE)
            part = jnp.sum(p.reshape(CHUNK // 8, 8, 256), axis=0)
            mix = jnp.dot(
                v_s[:, j * CHUNK:(j + 1) * CHUNK], p.astype(BF16), preferred_element_type=F32
            )
            acc = mix if acc is None else acc + mix
            total = part if total is None else total + part
        total = jnp.sum(total, axis=0, keepdims=True)
        o_ref, at = o_refs[h // 2], (h % 2) * STAT
        o_ref[at:at + 128] = (acc / total).astype(BF16)
        put_log(o_ref, at, top * EXP_SCALE + jnp.log2(total))


def attend(idx, qs, kv):
    shape = jax.ShapeDtypeStruct((2 * STAT, 256), BF16)
    return pl.pallas_call(
        attend_kernel,
        in_specs=[sspec()] + [vspec()] * 5,
        out_specs=[vspec()] * 4,
        out_shape=[shape] * 4,
        scratch_shapes=[
            VMEM((KEYS, 256), BF16), VMEM((128, KEYS), BF16), VMEM((128, 256), BF16),
            VMEM((KEYS, 256), F32), VMEM((KEYS, 256), F32),
        ],
        compiler_params=params(),
        cost_estimate=cost(4 * 2048 * 2048 * 128, 4 << 20, 2048 * 2048),
        name="attend",
    )(idx, *qs, kv)


def log_sum(ref, at):
    t = ref[at + 128:at + STAT].astype(F32)
    return t[0:1] + t[1:2] + t[2:3]


def put_log(ref, at, log):
    w = lax.broadcasted_iota(jnp.int32, (16, 256), 0)
    hi = log.astype(BF16).astype(F32)
    mid = (log - hi).astype(BF16).astype(F32)
    terms = jnp.where(w == 0, hi, jnp.where(w == 1, mid, jnp.where(w == 2, log - hi - mid, 0.0)))
    ref[at + 128:at + STAT] = terms.astype(BF16)


def merged(a_ref, b_ref, at):
    a, b = log_sum(a_ref, at), log_sum(b_ref, at)
    top = jnp.maximum(a, b)
    fa, fb = jnp.exp2(a - top), jnp.exp2(b - top)
    total = fa + fb
    mixed = a_ref[at:at + 128].astype(F32) * (fa / total)
    mixed = mixed + b_ref[at:at + 128].astype(F32) * (fb / total)
    return mixed, top + jnp.log2(total)


def merge_kernel(a0, a1, b0, b1, o0, o1):
    for a_ref, b_ref, o_ref in ((a0, b0, o0), (a1, b1, o1)):
        for h in range(2):
            at = h * STAT
            mixed, log = merged(a_ref, b_ref, at)
            o_ref[at:at + 128] = mixed.astype(BF16)
            put_log(o_ref, at, log)


def last_kernel(a0, a1, b0, b1, out_ref):
    for i, (a_ref, b_ref) in enumerate(((a0, b0), (a1, b1))):
        for h in range(2):
            mixed, _ = merged(a_ref, b_ref, h * STAT)
            col = (i * 2 + h) * 128
            out_ref[:, col:col + 128] = mixed.T.astype(BF16)


def place_kernel(idx, mine_ref, other_ref, out_ref):
    r = idx[3]
    for i in range(2):
        for mask, ref in ((0, mine_ref), (1, other_ref)):
            col = pl.multiple_of(((r ^ mask) ^ (i * 2)) * 256, 256)
            out_ref[:, pl.ds(col, 256)] = ref[:, i * 256:(i + 1) * 256]


def small(kernel, args, shapes, name, scalars=0):
    return pl.pallas_call(
        kernel,
        in_specs=[sspec()] * scalars + [vspec()] * (len(args) - scalars),
        out_specs=[vspec()] * len(shapes),
        out_shape=[jax.ShapeDtypeStruct(shape, BF16) for shape in shapes],
        compiler_params=params(),
        cost_estimate=cost(1 << 19, 1 << 20),
        name=name,
    )(*args)


REP = ("zl", "c")


def to_rep(x, mask):
    if mask == 1:
        return lax.ppermute(x, "c", SWAP)
    if mask == 2:
        return lax.ppermute(x, "zl", SWAP)
    return lax.ppermute(x, REP, [(i, i ^ mask) for i in range(4)])


def average(send, keep, zl, dtype):
    half = keep + lax.ppermute(send, "c", SWAP)
    mine = jnp.where(zl == 0, half[0], half[1])
    theirs = jnp.where(zl == 0, half[1], half[0]).astype(dtype)
    return mine, lax.ppermute(theirs, "zl", SWAP)


def local(tokens, query_ckpt, key_value_ckpt, numerators):
    zl, c, zh = lax.axis_index("zl"), lax.axis_index("c"), lax.axis_index("zh")
    f = lax.axis_index(("zh", "x", "y"))
    r = zl * 2 + c
    idx = jnp.stack([zh, c, f, r, lax.axis_index("x"), lax.axis_index("y")]).astype(jnp.int32)

    send, keep = prepare(idx, numerators, query_ckpt, key_value_ckpt)
    w_mine, w_got = average(send, keep, zl, BF16)

    scale, out = normalise(idx, tokens)
    out, w_got = lax.optimization_barrier((out, w_got))
    w = (w_mine + w_got.astype(F32)).astype(BF16)
    w_all = gather_plane(w)
    got = lax.ppermute(out, "zh", SWAP)
    got, *w_all = lax.optimization_barrier((got, *w_all))
    other = lax.ppermute(got, "c", SWAP)

    inverse_freq = jnp.exp(
        -(jnp.arange(64, dtype=F32) * (2.0 / HEAD)) * math.log(theta_base)
    )
    positions = (f * 256 + jnp.arange(256, dtype=jnp.int32)).astype(F32)
    angles = positions[:, None] * inverse_freq[None, :]
    cos, sin = jnp.cos(angles), jnp.sin(angles)
    my_freq = lax.dynamic_slice_in_dim(inverse_freq, r * 16, 16)
    angles_t = positions[None, :] * my_freq[:, None]
    cos_t, sin_t = jnp.cos(angles_t), jnp.sin(angles_t)

    (theirs,) = project(
        theirs_kernel, (idx, *w_all, got, other), [jax.ShapeDtypeStruct((384, 256), BF16)],
        "theirs")
    back = lax.ppermute(theirs, "zh", SWAP)
    q_own, pair_own = project(
        own_kernel, (idx, *w_all, tokens, scale),
        [jax.ShapeDtypeStruct((256, 256), F32), jax.ShapeDtypeStruct((64, 256), F32)], "own")
    pair = finish(
        pair_finish_kernel, (pair_own, back, cos_t, sin_t), (32, 4, 32, 128), "pair_finish")
    pair_all = lax.all_to_all(
        pair.reshape(128, 32, 128), ("zh", "x", "y", "zl", "c"), 0, 0)
    q0 = finish(q_finish_kernel, (q_own, back, cos, sin), (2, 128, 256), "q_finish")
    qs = [q0] + [to_rep(q0, m) for m in (1, 2, 3)]

    parts = attend(idx, qs, pair_all.reshape(32, 4, 32, 128))
    stat = (2 * STAT, 256)
    b0, b1 = to_rep(parts[1], 1), to_rep(parts[3], 1)
    a0, a1 = small(merge_kernel, (parts[0], parts[2], b0, b1), [stat, stat], "merge")
    c0, c1 = to_rep(a1, 2), to_rep(a0, 2)
    (mine,) = small(last_kernel, (a0, a1, c0, c1), [(256, 512)], "last")
    (out,) = small(place_kernel, (idx, mine, to_rep(mine, 1)), [(256, 1024)], "place", 1)
    return out


def solution(mesh):
    grid = Mesh(mesh.devices.reshape(2, 2, 2, 4, 4), ("zl", "c", "zh", "x", "y"))
    fsdp = ("zh", "x", "y")
    in_specs = (P(fsdp, None), P(REP, fsdp, None), P(REP, fsdp, None), P())
    return jax.shard_map(
        local, mesh=grid, in_specs=in_specs, out_specs=P(fsdp, None), check_vma=False
    )
```

```python
import functools
import math

import jax
import jax.numpy as jnp
from jax import lax
from jax.experimental import pallas as pl
from jax.experimental.pallas import tpu as pltpu
from jax.sharding import Mesh, PartitionSpec as P

theta_base = 500000.0
eps_norm = 1e-05
masked_score = -1e30
HEAD = 128
F32 = jnp.float32
BF16 = jnp.bfloat16
VMEM = pltpu.VMEM
SMEM = pltpu.SMEM
NT = (((1,), (1,)), ((), ()))
SWAP = [(0, 1), (1, 0)]


def params(mib=20):
    return pltpu.CompilerParams(vmem_limit_bytes=mib * 1024 * 1024)


def cost(flops, nbytes, trans=0):
    return pl.CostEstimate(flops=flops, bytes_accessed=nbytes, transcendentals=trans)


def vspec():
    return pl.BlockSpec(memory_space=VMEM)


def sspec():
    return pl.BlockSpec(memory_space=SMEM)


def pair_order():
    row = lax.broadcasted_iota(jnp.int32, (256, 256), 0)
    col = lax.broadcasted_iota(jnp.int32, (256, 256), 1)
    r, t = row // 64, row % 64
    key = r * 16 + t + jnp.where(t < 16, 0, 48)
    return jnp.where(col == jnp.where(t < 32, key, r * 32 + t + 96), 1.0, 0.0)


def norm_kernel(idx, x_ref, scale_ref, send_ref):
    zh, c = idx[0], idx[1]
    x = x_ref[...].astype(F32)
    scale = lax.rsqrt(jnp.mean(x * x, axis=-1, keepdims=True) + eps_norm)
    scale_ref[...] = jnp.broadcast_to(scale, scale_ref.shape)
    quarter = send_ref.shape[1]
    start = pl.multiple_of(((1 - zh) * 2 + c) * quarter, quarter)
    send_ref[...] = normed(x_ref, start, quarter, scale)


def normed(x_ref, start, width, scale):
    return (x_ref[:, pl.ds(start, width)].astype(F32) * scale).astype(BF16)


def normalise(idx, tokens):
    rows, width = tokens.shape
    step = 128
    return pl.pallas_call(
        norm_kernel,
        grid=(rows // step,),
        in_specs=[sspec(), pl.BlockSpec((step, width), lambda i: (i, 0))],
        out_specs=[
            pl.BlockSpec((step, 128), lambda i: (i, 0)),
            pl.BlockSpec((step, width // 4), lambda i: (i, 0)),
        ],
        out_shape=[
            jax.ShapeDtypeStruct((rows, 128), F32),
            jax.ShapeDtypeStruct((rows, width // 4), BF16),
        ],
        compiler_params=params(),
        cost_estimate=cost(rows * width * 4, rows * width * 3),
        name="normalise",
    )(idx, tokens)


def share_of(idx, num, shape):
    r = idx[3]
    total = num[0] + num[1] + num[2] + num[3]
    mine = jnp.full(shape, num[r], jnp.int32).astype(F32)
    return mine / jnp.full(shape, total, jnp.int32).astype(F32)


def prep_kernel(idx, num, q_ref, kv_ref, send_ref, keep_ref):
    c = idx[1]
    s = share_of(idx, num, (1, 256))
    kvt = lax.dot_general(
        pair_order(), kv_ref[0] * s, NT, precision=lax.Precision.HIGHEST,
        preferred_element_type=F32,
    )
    for zl in range(2):
        keep = pl.multiple_of((zl * 2 + c) * 256, 256)
        send = pl.multiple_of((zl * 2 + 1 - c) * 256, 256)
        first, second = kvt[zl * 128:zl * 128 + 64], kvt[zl * 128 + 64:zl * 128 + 128]
        for ref, col, pair in (
            (keep_ref, keep, jnp.where(c == 0, first, second)),
            (send_ref, send, jnp.where(c == 0, second, first)),
        ):
            for half in range(2):
                at = half * 160
                ref[zl, at:at + 128] = q_ref[0, half * 128:half * 128 + 128, pl.ds(col, 256)] * s
                ref[zl, at + 128:at + 160] = pair[half * 32:half * 32 + 32]


def prepare(idx, num, q, kv):
    shape = jax.ShapeDtypeStruct((2, 320, 256), F32)
    return pl.pallas_call(
        prep_kernel,
        in_specs=[sspec(), sspec()] + [vspec()] * 2,
        out_specs=[vspec(), vspec()],
        out_shape=[shape, shape],
        compiler_params=params(),
        cost_estimate=cost(1 << 20, 3 << 20),
        name="prepare",
    )(idx, num, q, kv)


def ring(step):
    return [(i, (i + step) % 4) for i in range(4)]


def gather_plane(w):
    lower, upper = w[0:160], w[160:320]
    lower = jnp.stack([lower] + [lax.ppermute(lower, "y", ring(d)) for d in (1, 3, 2)])
    upper = jnp.stack([upper] + [lax.ppermute(upper, "x", ring(d)) for d in (1, 3, 2)])
    lower, upper = lax.optimization_barrier((lower, upper))
    lowers = [lower] + [lax.ppermute(lower, "x", ring(d)) for d in (1, 3, 2)]
    uppers = [upper] + [lax.ppermute(upper, "y", ring(d)) for d in (1, 3, 2)]
    return lowers + uppers


def plane_block(idx, w_refs, j):
    back = (0, 1, 3, 2)
    dx, dy = j // 4, j % 4
    low, up = w_refs[dx], w_refs[4 + dy]
    q = jnp.concatenate([low[dy, 0:128], up[dx, 0:128]], axis=0)
    pair = jnp.concatenate([low[dy, 128:160], up[dx, 128:160]], axis=0)
    return q, pair, ((idx[4] + 4 - back[dx]) % 4) * 4 + (idx[5] + 4 - back[dy]) % 4


def accumulate(idx, w_refs, block):
    acc, pair_acc = None, None
    for j in range(16):
        w, pair, at = plane_block(idx, w_refs, j)
        x = block(at)
        part = jnp.dot(x, w, preferred_element_type=F32)
        pair_part = lax.dot_general(x, pair, NT, preferred_element_type=F32)
        acc = part if acc is None else acc + part
        pair_acc = pair_part if pair_acc is None else pair_acc + pair_part
    row = lax.broadcasted_iota(jnp.int32, (64, 64), 0)
    col = lax.broadcasted_iota(jnp.int32, (64, 64), 1)
    pair_acc = lax.dot_general(
        jnp.where(row == col, 1.0, 0.0), pair_acc, NT, precision=lax.Precision.HIGHEST,
        preferred_element_type=F32,
    )
    return acc, pair_acc


def own_kernel(idx, *refs):
    w_refs, (x_ref, scale_ref, q_ref, pair_ref) = refs[:-4], refs[-4:]
    scale = scale_ref[:, 0:1]

    def block(at):
        return normed(x_ref, pl.multiple_of((idx[0] * 16 + at) * 256, 256), 256, scale)

    q_ref[...], pair_ref[...] = accumulate(idx, w_refs, block)


def theirs_kernel(idx, *refs):
    w_refs, xa_ref, xb_refs, (out_ref, xb_ref) = refs[:8], refs[8], refs[9:-2], refs[-2:]
    width = xb_refs[0].shape[1]
    for i, ref in enumerate(xb_refs):
        xb_ref[:, i * width:(i + 1) * width] = ref[...]

    def block(at):
        cols = pl.ds(pl.multiple_of((at % 8) * 256, 256), 256)
        return jnp.where(at // 8 == idx[1], xa_ref[:, cols], xb_ref[:, cols])

    q, pair = accumulate(idx, w_refs, block)
    high = pair.astype(BF16)
    out_ref[0:256] = q.astype(BF16)
    out_ref[256:320] = high
    out_ref[320:384] = (pair - high.astype(F32)).astype(BF16)


def project(kernel, args, outs, name, scratch=()):
    return pl.pallas_call(
        kernel,
        scratch_shapes=scratch,
        in_specs=[sspec()] + [vspec()] * (len(args) - 1),
        out_specs=[vspec()] * len(outs),
        out_shape=outs,
        compiler_params=params(),
        cost_estimate=cost(2 * 256 * 320 * 4096, 5 << 20),
        name=name,
    )(*args)


def pair_finish_kernel(own_ref, got_ref, cos_ref, sin_ref, out_ref):
    t = own_ref[...] + (got_ref[256:320].astype(F32) + got_ref[320:384].astype(F32))
    u, w = t[0:16], t[16:32]
    cos, sin = cos_ref[...], sin_ref[...]
    key = jnp.concatenate([u * cos - w * sin, w * cos + u * sin], axis=0)
    val = t[32:64]
    for r in range(4):
        cols = slice(r * 64, (r + 1) * 64)
        piece = jnp.concatenate([key[:, cols], val[:, cols]], axis=1).astype(BF16)
        for f in range(out_ref.shape[0]):
            out_ref[f, r] = piece


def q_finish_kernel(own_ref, got_ref, cos_ref, sin_ref, out_ref):
    t = own_ref[...] + got_ref[0:256].astype(F32)
    cos, sin = cos_ref[...], sin_ref[...]
    for h in range(2):
        u = t[:, h * 128:h * 128 + 64]
        w = t[:, h * 128 + 64:h * 128 + 128]
        rotated = jnp.concatenate([u * cos - w * sin, w * cos + u * sin], axis=1)
        out_ref[h] = rotated.T.astype(BF16)


def finish(kernel, args, shape, name):
    return pl.pallas_call(
        kernel,
        in_specs=[vspec()] * 4,
        out_specs=vspec(),
        out_shape=jax.ShapeDtypeStruct(shape, BF16),
        compiler_params=params(),
        cost_estimate=cost(1 << 18, 1 << 20),
        name=name,
    )(*args)


CHUNK = 512
KEYS = 2048
EXP_SCALE = math.log2(math.e) / math.sqrt(HEAD)
STAT = 144


def attend_kernel(idx, *refs):
    q_refs, kv_ref = refs[0:4], refs[4]
    o_refs = refs[5:9]
    k_s, v_s, qx, s0, s1 = refs[9:]
    scores = (s0, s1)
    f, r = idx[2], idx[3]
    lane = lax.broadcasted_iota(jnp.int32, (32, 128), 1)
    col = lax.broadcasted_iota(jnp.int32, (128, 128), 1)
    row = lax.broadcasted_iota(jnp.int32, (128, 128), 0)
    for p in range(KEYS // 128):
        ks, vs = [], []
        for rr in range(4):
            a = kv_ref[2 * p, rr].astype(F32)
            b = kv_ref[2 * p + 1, rr].astype(F32)
            ks.append(jnp.where(lane < 64, a, pltpu.roll(b, 64, 1)).astype(BF16))
            vs.append(jnp.where(lane < 64, pltpu.roll(a, 64, 1), b).astype(BF16))
        key = jnp.concatenate([x[0:16] for x in ks] + [x[16:32] for x in ks], axis=0)
        k_s[p * 128:(p + 1) * 128, 0:128] = key.T
        blk = 2 * p + row // 64
        extra = jnp.where((blk == f) & (col == row % 64), 1.0, 0.0)
        extra = jnp.where((blk > f) & (col == 64), 1.0, extra)
        k_s[p * 128:(p + 1) * 128, 128:256] = extra.astype(BF16)
        v_s[:, p * 128:(p + 1) * 128] = jnp.concatenate(vs, axis=0)
    t = lax.broadcasted_iota(jnp.int32, (128, 256), 0)
    i = lax.broadcasted_iota(jnp.int32, (128, 256), 1)
    hidden = ((t < 64) & (64 * r + t > i)) | (t == 64)
    qx[...] = jnp.where(hidden, masked_score, 0.0).astype(BF16)

    def queries(h):
        return jnp.concatenate([q_refs[h // 2][h % 2], qx[...]], axis=0)

    def score(h, j, q, top):
        s = jnp.dot(k_s[j * CHUNK:(j + 1) * CHUNK], q, preferred_element_type=F32)
        scores[h % 2][j * CHUNK:(j + 1) * CHUNK] = s
        part = jnp.max(s.reshape(CHUNK // 8, 8, 256), axis=0)
        return part if top is None else jnp.maximum(top, part)

    chunks = KEYS // CHUNK
    tops, q = None, queries(0)
    for j in range(chunks):
        tops = score(0, j, q, tops)
    for h in range(8):
        top = jnp.max(tops, axis=0, keepdims=True)
        tops, acc, total = None, None, None
        if h < 7:
            q = queries(h + 1)
        for j in range(chunks):
            if h < 7:
                tops = score(h + 1, j, q, tops)
            p = jnp.exp2((scores[h % 2][j * CHUNK:(j + 1) * CHUNK] - top) * EXP_SCALE)
            part = jnp.sum(p.reshape(CHUNK // 8, 8, 256), axis=0)
            mix = jnp.dot(
                v_s[:, j * CHUNK:(j + 1) * CHUNK], p.astype(BF16), preferred_element_type=F32
            )
            acc = mix if acc is None else acc + mix
            total = part if total is None else total + part
        total = jnp.sum(total, axis=0, keepdims=True)
        o_ref, at = o_refs[h // 2], (h % 2) * STAT
        o_ref[at:at + 128] = (acc / total).astype(BF16)
        put_log(o_ref, at, top * EXP_SCALE + jnp.log2(total))


def attend(idx, qs, kv):
    shape = jax.ShapeDtypeStruct((2 * STAT, 256), BF16)
    return pl.pallas_call(
        attend_kernel,
        in_specs=[sspec()] + [vspec()] * 5,
        out_specs=[vspec()] * 4,
        out_shape=[shape] * 4,
        scratch_shapes=[
            VMEM((KEYS, 256), BF16), VMEM((128, KEYS), BF16), VMEM((128, 256), BF16),
            VMEM((KEYS, 256), F32), VMEM((KEYS, 256), F32),
        ],
        compiler_params=params(),
        cost_estimate=cost(4 * 2048 * 2048 * 128, 4 << 20, 2048 * 2048),
        name="attend",
    )(idx, *qs, kv)


def log_sum(ref, at):
    t = ref[at + 128:at + STAT].astype(F32)
    return t[0:1] + t[1:2] + t[2:3]


def put_log(ref, at, log):
    w = lax.broadcasted_iota(jnp.int32, (16, 256), 0)
    hi = log.astype(BF16).astype(F32)
    mid = (log - hi).astype(BF16).astype(F32)
    terms = jnp.where(w == 0, hi, jnp.where(w == 1, mid, jnp.where(w == 2, log - hi - mid, 0.0)))
    ref[at + 128:at + STAT] = terms.astype(BF16)


def merged(a_ref, b_ref, at):
    a, b = log_sum(a_ref, at), log_sum(b_ref, at)
    top = jnp.maximum(a, b)
    fa, fb = jnp.exp2(a - top), jnp.exp2(b - top)
    total = fa + fb
    mixed = a_ref[at:at + 128].astype(F32) * (fa / total)
    mixed = mixed + b_ref[at:at + 128].astype(F32) * (fb / total)
    return mixed, top + jnp.log2(total)


def merge_kernel(a0, a1, b0, b1, o0, o1):
    for a_ref, b_ref, o_ref in ((a0, b0, o0), (a1, b1, o1)):
        for h in range(2):
            at = h * STAT
            mixed, log = merged(a_ref, b_ref, at)
            o_ref[at:at + 128] = mixed.astype(BF16)
            put_log(o_ref, at, log)


def last_kernel(a0, a1, b0, b1, out_ref):
    for i, (a_ref, b_ref) in enumerate(((a0, b0), (a1, b1))):
        for h in range(2):
            mixed, _ = merged(a_ref, b_ref, h * STAT)
            col = (i * 2 + h) * 128
            out_ref[:, col:col + 128] = mixed.T.astype(BF16)


def place_kernel(idx, mine_ref, other_ref, out_ref):
    r = idx[3]
    for i in range(2):
        for mask, ref in ((0, mine_ref), (1, other_ref)):
            col = pl.multiple_of(((r ^ mask) ^ (i * 2)) * 256, 256)
            out_ref[:, pl.ds(col, 256)] = ref[:, i * 256:(i + 1) * 256]


def small(kernel, args, shapes, name, scalars=0):
    return pl.pallas_call(
        kernel,
        in_specs=[sspec()] * scalars + [vspec()] * (len(args) - scalars),
        out_specs=[vspec()] * len(shapes),
        out_shape=[jax.ShapeDtypeStruct(shape, BF16) for shape in shapes],
        compiler_params=params(),
        cost_estimate=cost(1 << 19, 1 << 20),
        name=name,
    )(*args)


REP = ("zl", "c")


def to_rep(x, mask):
    if mask == 1:
        return lax.ppermute(x, "c", SWAP)
    if mask == 2:
        return lax.ppermute(x, "zl", SWAP)
    return lax.ppermute(x, REP, [(i, i ^ mask) for i in range(4)])


def average(send, keep, zl, dtype):
    half = keep + lax.ppermute(send, "c", SWAP)
    mine = jnp.where(zl == 0, half[0], half[1])
    theirs = jnp.where(zl == 0, half[1], half[0]).astype(dtype)
    return mine, lax.ppermute(theirs, "zl", SWAP)


def local(tokens, query_ckpt, key_value_ckpt, numerators):
    zl, c, zh = lax.axis_index("zl"), lax.axis_index("c"), lax.axis_index("zh")
    f = lax.axis_index(("zh", "x", "y"))
    r = zl * 2 + c
    idx = jnp.stack([zh, c, f, r, lax.axis_index("x"), lax.axis_index("y")]).astype(jnp.int32)

    send, keep = prepare(idx, numerators, query_ckpt, key_value_ckpt)
    w_mine, w_got = average(send, keep, zl, BF16)

    scale, out = normalise(idx, tokens)
    out, w_got = lax.optimization_barrier((out, w_got))
    w = (w_mine + w_got.astype(F32)).astype(BF16)
    w_all = gather_plane(w)
    got = lax.ppermute(out, "zh", SWAP)
    width = got.shape[1] // 4
    other = [lax.ppermute(got[:, i * width:(i + 1) * width], "c", SWAP) for i in range(4)]

    inverse_freq = jnp.exp(
        -(jnp.arange(64, dtype=F32) * (2.0 / HEAD)) * math.log(theta_base)
    )
    positions = (f * 256 + jnp.arange(256, dtype=jnp.int32)).astype(F32)
    angles = positions[:, None] * inverse_freq[None, :]
    cos, sin = jnp.cos(angles), jnp.sin(angles)
    my_freq = lax.dynamic_slice_in_dim(inverse_freq, r * 16, 16)
    angles_t = positions[None, :] * my_freq[:, None]
    cos_t, sin_t = jnp.cos(angles_t), jnp.sin(angles_t)

    (theirs,) = project(
        theirs_kernel, (idx, *w_all, got, *other), [jax.ShapeDtypeStruct((384, 256), BF16)],
        "theirs", [VMEM((256, 2048), BF16)])
    back = lax.ppermute(theirs, "zh", SWAP)
    q_own, pair_own = project(
        own_kernel, (idx, *w_all, tokens, scale),
        [jax.ShapeDtypeStruct((256, 256), F32), jax.ShapeDtypeStruct((64, 256), F32)], "own")
    pair = finish(
        pair_finish_kernel, (pair_own, back, cos_t, sin_t), (32, 4, 32, 128), "pair_finish")
    pair_all = lax.all_to_all(
        pair.reshape(128, 32, 128), ("zh", "x", "y", "zl", "c"), 0, 0)
    q0 = finish(q_finish_kernel, (q_own, back, cos, sin), (2, 128, 256), "q_finish")
    q1, q2 = to_rep(q0, 1), to_rep(q0, 2)
    qs = [q0, q1, q2, to_rep(q2, 1)]

    parts = attend(idx, qs, pair_all.reshape(32, 4, 32, 128))
    stat = (2 * STAT, 256)
    b0, b1 = to_rep(parts[1], 1), to_rep(parts[3], 1)
    a0, a1 = small(merge_kernel, (parts[0], parts[2], b0, b1), [stat, stat], "merge")
    c0, c1 = to_rep(a1, 2), to_rep(a0, 2)
    (mine,) = small(last_kernel, (a0, a1, c0, c1), [(256, 512)], "last")
    (out,) = small(place_kernel, (idx, mine, to_rep(mine, 1)), [(256, 1024)], "place", 1)
    return out


def solution(mesh):
    grid = Mesh(mesh.devices.reshape(2, 2, 2, 4, 4), ("zl", "c", "zh", "x", "y"))
    fsdp = ("zh", "x", "y")
    in_specs = (P(fsdp, None), P(REP, fsdp, None), P(REP, fsdp, None), P())
    return jax.shard_map(
        local, mesh=grid, in_specs=in_specs, out_specs=P(fsdp, None), check_vma=False
    )
```

```python
import functools
import math

import jax
import jax.numpy as jnp
from jax import lax
from jax.experimental import pallas as pl
from jax.experimental.pallas import tpu as pltpu
from jax.sharding import Mesh, PartitionSpec as P

theta_base = 500000.0
eps_norm = 1e-05
masked_score = -1e30
HEAD = 128
F32 = jnp.float32
BF16 = jnp.bfloat16
VMEM = pltpu.VMEM
SMEM = pltpu.SMEM
NT = (((1,), (1,)), ((), ()))
SWAP = [(0, 1), (1, 0)]


def params(mib=20):
    return pltpu.CompilerParams(vmem_limit_bytes=mib * 1024 * 1024)


def cost(flops, nbytes, trans=0):
    return pl.CostEstimate(flops=flops, bytes_accessed=nbytes, transcendentals=trans)


def vspec():
    return pl.BlockSpec(memory_space=VMEM)


def sspec():
    return pl.BlockSpec(memory_space=SMEM)


def pair_order():
    row = lax.broadcasted_iota(jnp.int32, (256, 256), 0)
    col = lax.broadcasted_iota(jnp.int32, (256, 256), 1)
    r, t = row // 64, row % 64
    key = r * 16 + t + jnp.where(t < 16, 0, 48)
    return jnp.where(col == jnp.where(t < 32, key, r * 32 + t + 96), 1.0, 0.0)


def norm_kernel(idx, x_ref, scale_ref, send_ref):
    zh, c = idx[0], idx[1]
    x = x_ref[...].astype(F32)
    scale = lax.rsqrt(jnp.mean(x * x, axis=-1, keepdims=True) + eps_norm)
    scale_ref[...] = jnp.broadcast_to(scale, scale_ref.shape)
    quarter = send_ref.shape[1]
    start = pl.multiple_of(((1 - zh) * 2 + c) * quarter, quarter)
    send_ref[...] = normed(x_ref, start, quarter, scale)


def normed(x_ref, start, width, scale):
    return (x_ref[:, pl.ds(start, width)].astype(F32) * scale).astype(BF16)


def normalise(idx, tokens):
    rows, width = tokens.shape
    step = 128
    return pl.pallas_call(
        norm_kernel,
        grid=(rows // step,),
        in_specs=[sspec(), pl.BlockSpec((step, width), lambda i: (i, 0))],
        out_specs=[
            pl.BlockSpec((step, 128), lambda i: (i, 0)),
            pl.BlockSpec((step, width // 4), lambda i: (i, 0)),
        ],
        out_shape=[
            jax.ShapeDtypeStruct((rows, 128), F32),
            jax.ShapeDtypeStruct((rows, width // 4), BF16),
        ],
        compiler_params=params(),
        cost_estimate=cost(rows * width * 4, rows * width * 3),
        name="normalise",
    )(idx, tokens)


def share_of(idx, num, shape):
    r = idx[3]
    total = num[0] + num[1] + num[2] + num[3]
    mine = jnp.full(shape, num[r], jnp.int32).astype(F32)
    return mine / jnp.full(shape, total, jnp.int32).astype(F32)


def prep_kernel(idx, num, q_ref, kv_ref, send_ref, keep_ref):
    c = idx[1]
    s = share_of(idx, num, (1, 256))
    kvt = lax.dot_general(
        pair_order(), kv_ref[0] * s, NT, precision=lax.Precision.HIGHEST,
        preferred_element_type=F32,
    )
    for zl in range(2):
        keep = pl.multiple_of((zl * 2 + c) * 256, 256)
        send = pl.multiple_of((zl * 2 + 1 - c) * 256, 256)
        first, second = kvt[zl * 128:zl * 128 + 64], kvt[zl * 128 + 64:zl * 128 + 128]
        for ref, col, pair in (
            (keep_ref, keep, jnp.where(c == 0, first, second)),
            (send_ref, send, jnp.where(c == 0, second, first)),
        ):
            for half in range(2):
                at = half * 160
                ref[zl, at:at + 128] = q_ref[0, half * 128:half * 128 + 128, pl.ds(col, 256)] * s
                ref[zl, at + 128:at + 160] = pair[half * 32:half * 32 + 32]


def prepare(idx, num, q, kv):
    shape = jax.ShapeDtypeStruct((2, 320, 256), F32)
    return pl.pallas_call(
        prep_kernel,
        in_specs=[sspec(), sspec()] + [vspec()] * 2,
        out_specs=[vspec(), vspec()],
        out_shape=[shape, shape],
        compiler_params=params(),
        cost_estimate=cost(1 << 20, 3 << 20),
        name="prepare",
    )(idx, num, q, kv)


def ring(step):
    return [(i, (i + step) % 4) for i in range(4)]


def gather_plane(w):
    lower, upper = w[0:160], w[160:320]
    lower = jnp.stack([lower] + [lax.ppermute(lower, "y", ring(d)) for d in (1, 3, 2)])
    upper = jnp.stack([upper] + [lax.ppermute(upper, "x", ring(d)) for d in (1, 3, 2)])
    lower, upper = lax.optimization_barrier((lower, upper))
    lowers = [lower] + [lax.ppermute(lower, "x", ring(d)) for d in (1, 3, 2)]
    uppers = [upper] + [lax.ppermute(upper, "y", ring(d)) for d in (1, 3, 2)]
    return lowers + uppers


def plane_block(idx, w_refs, j):
    back = (0, 1, 3, 2)
    dx, dy = j // 4, j % 4
    low, up = w_refs[dx], w_refs[4 + dy]
    q = jnp.concatenate([low[dy, 0:128], up[dx, 0:128]], axis=0)
    pair = jnp.concatenate([low[dy, 128:160], up[dx, 128:160]], axis=0)
    return q, pair, ((idx[4] + 4 - back[dx]) % 4) * 4 + (idx[5] + 4 - back[dy]) % 4


def accumulate(idx, w_refs, block):
    acc, pair_acc = None, None
    for j in range(16):
        w, pair, at = plane_block(idx, w_refs, j)
        x = block(at)
        part = jnp.dot(x, w, preferred_element_type=F32)
        pair_part = lax.dot_general(x, pair, NT, preferred_element_type=F32)
        acc = part if acc is None else acc + part
        pair_acc = pair_part if pair_acc is None else pair_acc + pair_part
    row = lax.broadcasted_iota(jnp.int32, (64, 64), 0)
    col = lax.broadcasted_iota(jnp.int32, (64, 64), 1)
    pair_acc = lax.dot_general(
        jnp.where(row == col, 1.0, 0.0), pair_acc, NT, precision=lax.Precision.HIGHEST,
        preferred_element_type=F32,
    )
    return acc, pair_acc


def own_kernel(idx, *refs):
    w_refs, (x_ref, scale_ref, q_ref, pair_ref) = refs[:-4], refs[-4:]
    scale = scale_ref[:, 0:1]

    def block(at):
        return normed(x_ref, pl.multiple_of((idx[0] * 16 + at) * 256, 256), 256, scale)

    q_ref[...], pair_ref[...] = accumulate(idx, w_refs, block)


def theirs_kernel(idx, *refs):
    w_refs, xa_ref, xb_refs, (out_ref, xb_ref) = refs[:8], refs[8], refs[9:-2], refs[-2:]
    width = xb_refs[0].shape[1]
    for i, ref in enumerate(xb_refs):
        xb_ref[:, i * width:(i + 1) * width] = ref[...]

    def block(at):
        cols = pl.ds(pl.multiple_of((at % 8) * 256, 256), 256)
        return jnp.where(at // 8 == idx[1], xa_ref[:, cols], xb_ref[:, cols])

    q, pair = accumulate(idx, w_refs, block)
    out_ref[0:256] = q.astype(BF16)
    out_ref[256:320] = pair.astype(BF16)


def project(kernel, args, outs, name, scratch=()):
    return pl.pallas_call(
        kernel,
        scratch_shapes=scratch,
        in_specs=[sspec()] + [vspec()] * (len(args) - 1),
        out_specs=[vspec()] * len(outs),
        out_shape=outs,
        compiler_params=params(),
        cost_estimate=cost(2 * 256 * 320 * 4096, 5 << 20),
        name=name,
    )(*args)


def pair_finish_kernel(own_ref, got_ref, cos_ref, sin_ref, out_ref):
    t = own_ref[...] + got_ref[256:320].astype(F32)
    u, w = t[0:16], t[16:32]
    cos, sin = cos_ref[...], sin_ref[...]
    key = jnp.concatenate([u * cos - w * sin, w * cos + u * sin], axis=0)
    val = t[32:64]
    for r in range(4):
        cols = slice(r * 64, (r + 1) * 64)
        piece = jnp.concatenate([key[:, cols], val[:, cols]], axis=1).astype(BF16)
        for f in range(out_ref.shape[0]):
            out_ref[f, r] = piece


def q_finish_kernel(own_ref, got_ref, cos_ref, sin_ref, out_ref):
    t = own_ref[...] + got_ref[0:256].astype(F32)
    cos, sin = cos_ref[...], sin_ref[...]
    for h in range(2):
        u = t[:, h * 128:h * 128 + 64]
        w = t[:, h * 128 + 64:h * 128 + 128]
        rotated = jnp.concatenate([u * cos - w * sin, w * cos + u * sin], axis=1)
        out_ref[h] = rotated.T.astype(BF16)


def finish(kernel, args, shape, name):
    return pl.pallas_call(
        kernel,
        in_specs=[vspec()] * 4,
        out_specs=vspec(),
        out_shape=jax.ShapeDtypeStruct(shape, BF16),
        compiler_params=params(),
        cost_estimate=cost(1 << 18, 1 << 20),
        name=name,
    )(*args)


CHUNK = 512
KEYS = 2048
EXP_SCALE = math.log2(math.e) / math.sqrt(HEAD)
STAT = 144


def attend_kernel(idx, *refs):
    q_refs, kv_ref = refs[0:4], refs[4]
    o_refs = refs[5:7]
    k_s, v_s, qx, s0, s1 = refs[7:]
    scores = (s0, s1)
    f, r = idx[2], idx[3]
    lane = lax.broadcasted_iota(jnp.int32, (32, 128), 1)
    col = lax.broadcasted_iota(jnp.int32, (128, 128), 1)
    row = lax.broadcasted_iota(jnp.int32, (128, 128), 0)
    for p in range(KEYS // 128):
        ks, vs = [], []
        for rr in range(4):
            a = kv_ref[2 * p, rr].astype(F32)
            b = kv_ref[2 * p + 1, rr].astype(F32)
            ks.append(jnp.where(lane < 64, a, pltpu.roll(b, 64, 1)).astype(BF16))
            vs.append(jnp.where(lane < 64, pltpu.roll(a, 64, 1), b).astype(BF16))
        key = jnp.concatenate([x[0:16] for x in ks] + [x[16:32] for x in ks], axis=0)
        k_s[p * 128:(p + 1) * 128, 0:128] = key.T
        blk = 2 * p + row // 64
        extra = jnp.where((blk == f) & (col == row % 64), 1.0, 0.0)
        extra = jnp.where((blk > f) & (col == 64), 1.0, extra)
        k_s[p * 128:(p + 1) * 128, 128:256] = extra.astype(BF16)
        v_s[:, p * 128:(p + 1) * 128] = jnp.concatenate(vs, axis=0)
    t = lax.broadcasted_iota(jnp.int32, (128, 256), 0)
    i = lax.broadcasted_iota(jnp.int32, (128, 256), 1)
    hidden = ((t < 64) & (64 * r + t > i)) | (t == 64)
    qx[...] = jnp.where(hidden, masked_score, 0.0).astype(BF16)

    def queries(h):
        return jnp.concatenate([q_refs[h // 2][h % 2], qx[...]], axis=0)

    def score(h, j, q, top):
        s = jnp.dot(k_s[j * CHUNK:(j + 1) * CHUNK], q, preferred_element_type=F32)
        scores[h % 2][j * CHUNK:(j + 1) * CHUNK] = s
        part = jnp.max(s.reshape(CHUNK // 8, 8, 256), axis=0)
        return part if top is None else jnp.maximum(top, part)

    chunks = KEYS // CHUNK
    tops, q = None, queries(0)
    for j in range(chunks):
        tops = score(0, j, q, tops)
    for h in range(8):
        top = jnp.max(tops, axis=0, keepdims=True)
        tops, acc, total = None, None, None
        if h < 7:
            q = queries(h + 1)
        for j in range(chunks):
            if h < 7:
                tops = score(h + 1, j, q, tops)
            p = jnp.exp2((scores[h % 2][j * CHUNK:(j + 1) * CHUNK] - top) * EXP_SCALE)
            part = jnp.sum(p.reshape(CHUNK // 8, 8, 256), axis=0)
            mix = jnp.dot(
                v_s[:, j * CHUNK:(j + 1) * CHUNK], p.astype(BF16), preferred_element_type=F32
            )
            acc = mix if acc is None else acc + mix
            total = part if total is None else total + part
        total = jnp.sum(total, axis=0, keepdims=True)
        o_ref, at = o_refs[h // 2 % 2], (h // 4 * 2 + h % 2) * STAT
        o_ref[at:at + 128] = (acc / total).astype(BF16)
        put_log(o_ref, at, top * EXP_SCALE + jnp.log2(total))


def attend(idx, qs, kv):
    shape = jax.ShapeDtypeStruct((4 * STAT, 256), BF16)
    return pl.pallas_call(
        attend_kernel,
        in_specs=[sspec()] + [vspec()] * 5,
        out_specs=[vspec()] * 2,
        out_shape=[shape] * 2,
        scratch_shapes=[
            VMEM((KEYS, 256), BF16), VMEM((128, KEYS), BF16), VMEM((128, 256), BF16),
            VMEM((KEYS, 256), F32), VMEM((KEYS, 256), F32),
        ],
        compiler_params=params(),
        cost_estimate=cost(4 * 2048 * 2048 * 128, 4 << 20, 2048 * 2048),
        name="attend",
    )(idx, *qs, kv)


def log_sum(ref, at):
    t = ref[at + 128:at + STAT].astype(F32)
    return t[0:1] + t[1:2] + t[2:3]


def put_log(ref, at, log):
    w = lax.broadcasted_iota(jnp.int32, (16, 256), 0)
    hi = log.astype(BF16).astype(F32)
    mid = (log - hi).astype(BF16).astype(F32)
    terms = jnp.where(w == 0, hi, jnp.where(w == 1, mid, jnp.where(w == 2, log - hi - mid, 0.0)))
    ref[at + 128:at + STAT] = terms.astype(BF16)


def merged(a_ref, b_ref, i, j):
    a, b = log_sum(a_ref, i), log_sum(b_ref, j)
    top = jnp.maximum(a, b)
    fa, fb = jnp.exp2(a - top), jnp.exp2(b - top)
    total = fa + fb
    mixed = a_ref[i:i + 128].astype(F32) * (fa / total)
    mixed = mixed + b_ref[j:j + 128].astype(F32) * (fb / total)
    return mixed, top + jnp.log2(total)


def merge_kernel(a_ref, b_ref, o_ref):
    for h in range(4):
        at = h * STAT
        mixed, log = merged(a_ref, b_ref, at, at)
        o_ref[at:at + 128] = mixed.astype(BF16)
        put_log(o_ref, at, log)


def last_kernel(a_ref, b_ref, out_ref):
    for h in range(4):
        mixed, _ = merged(a_ref, b_ref, h * STAT, (h + 2) % 4 * STAT)
        out_ref[:, h * 128:(h + 1) * 128] = mixed.T.astype(BF16)


def place_kernel(idx, mine_ref, other_ref, out_ref):
    r = idx[3]
    for i in range(2):
        for mask, ref in ((0, mine_ref), (1, other_ref)):
            col = pl.multiple_of(((r ^ mask) ^ (i * 2)) * 256, 256)
            out_ref[:, pl.ds(col, 256)] = ref[:, i * 256:(i + 1) * 256]


def small(kernel, args, shapes, name, scalars=0):
    return pl.pallas_call(
        kernel,
        in_specs=[sspec()] * scalars + [vspec()] * (len(args) - scalars),
        out_specs=[vspec()] * len(shapes),
        out_shape=[jax.ShapeDtypeStruct(shape, BF16) for shape in shapes],
        compiler_params=params(),
        cost_estimate=cost(1 << 19, 1 << 20),
        name=name,
    )(*args)


REP = ("zl", "c")


def to_rep(x, mask):
    if mask == 1:
        return lax.ppermute(x, "c", SWAP)
    if mask == 2:
        return lax.ppermute(x, "zl", SWAP)
    return lax.ppermute(x, REP, [(i, i ^ mask) for i in range(4)])


def average(send, keep, zl, dtype):
    half = keep + lax.ppermute(send, "c", SWAP)
    mine = jnp.where(zl == 0, half[0], half[1])
    theirs = jnp.where(zl == 0, half[1], half[0]).astype(dtype)
    return mine, lax.ppermute(theirs, "zl", SWAP)


def local(tokens, query_ckpt, key_value_ckpt, numerators):
    zl, c, zh = lax.axis_index("zl"), lax.axis_index("c"), lax.axis_index("zh")
    f = lax.axis_index(("zh", "x", "y"))
    r = zl * 2 + c
    idx = jnp.stack([zh, c, f, r, lax.axis_index("x"), lax.axis_index("y")]).astype(jnp.int32)

    send, keep = prepare(idx, numerators, query_ckpt, key_value_ckpt)
    w_mine, w_got = average(send, keep, zl, BF16)

    scale, out = normalise(idx, tokens)
    out, w_got = lax.optimization_barrier((out, w_got))
    w = (w_mine + w_got.astype(F32)).astype(BF16)
    w_all = gather_plane(w)
    got = lax.ppermute(out, "zh", SWAP)
    width = got.shape[1] // 4
    other = [lax.ppermute(got[:, i * width:(i + 1) * width], "c", SWAP) for i in range(4)]

    inverse_freq = jnp.exp(
        -(jnp.arange(64, dtype=F32) * (2.0 / HEAD)) * math.log(theta_base)
    )
    positions = (f * 256 + jnp.arange(256, dtype=jnp.int32)).astype(F32)
    angles = positions[:, None] * inverse_freq[None, :]
    cos, sin = jnp.cos(angles), jnp.sin(angles)
    my_freq = lax.dynamic_slice_in_dim(inverse_freq, r * 16, 16)
    angles_t = positions[None, :] * my_freq[:, None]
    cos_t, sin_t = jnp.cos(angles_t), jnp.sin(angles_t)

    (theirs,) = project(
        theirs_kernel, (idx, *w_all, got, *other), [jax.ShapeDtypeStruct((320, 256), BF16)],
        "theirs", [VMEM((256, 2048), BF16)])
    back = lax.ppermute(theirs, "zh", SWAP)
    q_own, pair_own = project(
        own_kernel, (idx, *w_all, tokens, scale),
        [jax.ShapeDtypeStruct((256, 256), F32), jax.ShapeDtypeStruct((64, 256), F32)], "own")
    pair = finish(
        pair_finish_kernel, (pair_own, back, cos_t, sin_t), (32, 4, 32, 128), "pair_finish")
    pair_all = lax.all_to_all(
        pair.reshape(128, 32, 128), ("zh", "x", "y", "zl", "c"), 0, 0)
    q0 = finish(q_finish_kernel, (q_own, back, cos, sin), (2, 128, 256), "q_finish")
    q1, q2 = to_rep(q0, 1), to_rep(q0, 2)
    qs = [q0, q1, q2, to_rep(q2, 1)]

    kept, sent = attend(idx, qs, pair_all.reshape(32, 4, 32, 128))
    (part,) = small(merge_kernel, (kept, to_rep(sent, 1)), [(4 * STAT, 256)], "merge")
    (mine,) = small(last_kernel, (part, to_rep(part, 2)), [(256, 512)], "last")
    (out,) = small(place_kernel, (idx, mine, to_rep(mine, 1)), [(256, 1024)], "place", 1)
    return out


def solution(mesh):
    grid = Mesh(mesh.devices.reshape(2, 2, 2, 4, 4), ("zl", "c", "zh", "x", "y"))
    fsdp = ("zh", "x", "y")
    in_specs = (P(fsdp, None), P(REP, fsdp, None), P(REP, fsdp, None), P())
    return jax.shard_map(
        local, mesh=grid, in_specs=in_specs, out_specs=P(fsdp, None), check_vma=False
    )
```

```python
import functools
import math

import jax
import jax.numpy as jnp
from jax import lax
from jax.experimental import pallas as pl
from jax.experimental.pallas import tpu as pltpu
from jax.sharding import Mesh, PartitionSpec as P

theta_base = 500000.0
eps_norm = 1e-05
masked_score = -1e30
HEAD = 128
F32 = jnp.float32
BF16 = jnp.bfloat16
VMEM = pltpu.VMEM
SMEM = pltpu.SMEM
NT = (((1,), (1,)), ((), ()))
SWAP = [(0, 1), (1, 0)]


def params(mib=20):
    return pltpu.CompilerParams(vmem_limit_bytes=mib * 1024 * 1024)


def cost(flops, nbytes, trans=0):
    return pl.CostEstimate(flops=flops, bytes_accessed=nbytes, transcendentals=trans)


def vspec():
    return pl.BlockSpec(memory_space=VMEM)


def sspec():
    return pl.BlockSpec(memory_space=SMEM)


def pair_order():
    row = lax.broadcasted_iota(jnp.int32, (256, 256), 0)
    col = lax.broadcasted_iota(jnp.int32, (256, 256), 1)
    r, t = row // 64, row % 64
    key = r * 16 + t + jnp.where(t < 16, 0, 48)
    return jnp.where(col == jnp.where(t < 32, key, r * 32 + t + 96), 1.0, 0.0)


def norm_kernel(idx, x_ref, scale_ref, send_ref):
    zh, c = idx[0], idx[1]
    x = x_ref[...].astype(F32)
    scale = lax.rsqrt(jnp.mean(x * x, axis=-1, keepdims=True) + eps_norm)
    scale_ref[...] = jnp.broadcast_to(scale, scale_ref.shape)
    quarter = send_ref.shape[1]
    start = pl.multiple_of(((1 - zh) * 2 + c) * quarter, quarter)
    send_ref[...] = normed(x_ref, start, quarter, scale)


def normed(x_ref, start, width, scale):
    return (x_ref[:, pl.ds(start, width)].astype(F32) * scale).astype(BF16)


def normalise(idx, tokens):
    rows, width = tokens.shape
    step = 128
    return pl.pallas_call(
        norm_kernel,
        grid=(rows // step,),
        in_specs=[sspec(), pl.BlockSpec((step, width), lambda i: (i, 0))],
        out_specs=[
            pl.BlockSpec((step, 128), lambda i: (i, 0)),
            pl.BlockSpec((step, width // 4), lambda i: (i, 0)),
        ],
        out_shape=[
            jax.ShapeDtypeStruct((rows, 128), F32),
            jax.ShapeDtypeStruct((rows, width // 4), BF16),
        ],
        compiler_params=params(),
        cost_estimate=cost(rows * width * 4, rows * width * 3),
        name="normalise",
    )(idx, tokens)


def share_of(idx, num, shape):
    r = idx[3]
    total = num[0] + num[1] + num[2] + num[3]
    mine = jnp.full(shape, num[r], jnp.int32).astype(F32)
    return mine / jnp.full(shape, total, jnp.int32).astype(F32)


def prep_kernel(idx, num, q_ref, kv_ref, send_ref, keep_ref):
    c = idx[1]
    s = share_of(idx, num, (1, 256))
    kvt = lax.dot_general(
        pair_order(), kv_ref[0] * s, NT, precision=lax.Precision.HIGHEST,
        preferred_element_type=F32,
    )
    for zl in range(2):
        keep = pl.multiple_of((zl * 2 + c) * 256, 256)
        send = pl.multiple_of((zl * 2 + 1 - c) * 256, 256)
        first, second = kvt[zl * 128:zl * 128 + 64], kvt[zl * 128 + 64:zl * 128 + 128]
        for ref, col, pair in (
            (keep_ref, keep, jnp.where(c == 0, first, second)),
            (send_ref, send, jnp.where(c == 0, second, first)),
        ):
            for half in range(2):
                at = half * 160
                ref[zl, at:at + 128] = q_ref[0, half * 128:half * 128 + 128, pl.ds(col, 256)] * s
                ref[zl, at + 128:at + 160] = pair[half * 32:half * 32 + 32]


def prepare(idx, num, q, kv):
    shape = jax.ShapeDtypeStruct((2, 320, 256), F32)
    return pl.pallas_call(
        prep_kernel,
        in_specs=[sspec(), sspec()] + [vspec()] * 2,
        out_specs=[vspec(), vspec()],
        out_shape=[shape, shape],
        compiler_params=params(),
        cost_estimate=cost(1 << 20, 3 << 20),
        name="prepare",
    )(idx, num, q, kv)


def ring(step):
    return [(i, (i + step) % 4) for i in range(4)]


def gather_plane(w):
    lower, upper = w[0:160], w[160:320]
    lower = jnp.stack([lower] + [lax.ppermute(lower, "y", ring(d)) for d in (1, 3, 2)])
    upper = jnp.stack([upper] + [lax.ppermute(upper, "x", ring(d)) for d in (1, 3, 2)])
    lower, upper = lax.optimization_barrier((lower, upper))
    lowers = [lower] + [lax.ppermute(lower, "x", ring(d)) for d in (1, 3, 2)]
    uppers = [upper] + [lax.ppermute(upper, "y", ring(d)) for d in (1, 3, 2)]
    return lowers + uppers


def plane_block(idx, w_refs, j):
    back = (0, 1, 3, 2)
    dx, dy = j // 4, j % 4
    low, up = w_refs[dx], w_refs[4 + dy]
    q = jnp.concatenate([low[dy, 0:128], up[dx, 0:128]], axis=0)
    pair = jnp.concatenate([low[dy, 128:160], up[dx, 128:160]], axis=0)
    return q, pair, ((idx[4] + 4 - back[dx]) % 4) * 4 + (idx[5] + 4 - back[dy]) % 4


def accumulate(idx, w_refs, block):
    acc, pair_acc = None, None
    for j in range(16):
        w, pair, at = plane_block(idx, w_refs, j)
        x = block(at)
        part = jnp.dot(x, w, preferred_element_type=F32)
        pair_part = lax.dot_general(x, pair, NT, preferred_element_type=F32)
        acc = part if acc is None else acc + part
        pair_acc = pair_part if pair_acc is None else pair_acc + pair_part
    row = lax.broadcasted_iota(jnp.int32, (64, 64), 0)
    col = lax.broadcasted_iota(jnp.int32, (64, 64), 1)
    pair_acc = lax.dot_general(
        jnp.where(row == col, 1.0, 0.0), pair_acc, NT, precision=lax.Precision.HIGHEST,
        preferred_element_type=F32,
    )
    return acc, pair_acc


def own_kernel(idx, *refs):
    w_refs, (x_ref, scale_ref, q_ref, pair_ref) = refs[:-4], refs[-4:]
    scale = scale_ref[:, 0:1]

    def block(at):
        return normed(x_ref, pl.multiple_of((idx[0] * 16 + at) * 256, 256), 256, scale)

    q_ref[...], pair_ref[...] = accumulate(idx, w_refs, block)


def theirs_kernel(idx, *refs):
    w_refs, xa_ref, xb_refs, (out_ref, xb_ref) = refs[:8], refs[8], refs[9:-2], refs[-2:]
    width = xb_refs[0].shape[1]
    for i, ref in enumerate(xb_refs):
        xb_ref[:, i * width:(i + 1) * width] = ref[...]

    def block(at):
        cols = pl.ds(pl.multiple_of((at % 8) * 256, 256), 256)
        return jnp.where(at // 8 == idx[1], xa_ref[:, cols], xb_ref[:, cols])

    q, pair = accumulate(idx, w_refs, block)
    high = pair.astype(BF16)
    out_ref[0:256] = q.astype(BF16)
    out_ref[256:320] = high
    out_ref[320:384] = (pair - high.astype(F32)).astype(BF16)


def project(kernel, args, outs, name, scratch=()):
    return pl.pallas_call(
        kernel,
        scratch_shapes=scratch,
        in_specs=[sspec()] + [vspec()] * (len(args) - 1),
        out_specs=[vspec()] * len(outs),
        out_shape=outs,
        compiler_params=params(),
        cost_estimate=cost(2 * 256 * 320 * 4096, 5 << 20),
        name=name,
    )(*args)


def pair_finish_kernel(own_ref, got_ref, cos_ref, sin_ref, out_ref):
    t = own_ref[...] + (got_ref[256:320].astype(F32) + got_ref[320:384].astype(F32))
    u, w = t[0:16], t[16:32]
    cos, sin = cos_ref[...], sin_ref[...]
    key = jnp.concatenate([u * cos - w * sin, w * cos + u * sin], axis=0)
    val = t[32:64]
    for r in range(4):
        cols = slice(r * 64, (r + 1) * 64)
        piece = jnp.concatenate([key[:, cols], val[:, cols]], axis=1).astype(BF16)
        for f in range(out_ref.shape[0]):
            out_ref[f, r] = piece


def q_finish_kernel(own_ref, got_ref, cos_ref, sin_ref, out_ref):
    t = own_ref[...] + got_ref[0:256].astype(F32)
    cos, sin = cos_ref[...], sin_ref[...]
    for h in range(2):
        u = t[:, h * 128:h * 128 + 64]
        w = t[:, h * 128 + 64:h * 128 + 128]
        rotated = jnp.concatenate([u * cos - w * sin, w * cos + u * sin], axis=1)
        out_ref[h] = rotated.T.astype(BF16)


def finish(kernel, args, shape, name):
    return pl.pallas_call(
        kernel,
        in_specs=[vspec()] * 4,
        out_specs=vspec(),
        out_shape=jax.ShapeDtypeStruct(shape, BF16),
        compiler_params=params(),
        cost_estimate=cost(1 << 18, 1 << 20),
        name=name,
    )(*args)


CHUNK = 512
KEYS = 2048
EXP_SCALE = math.log2(math.e) / math.sqrt(HEAD)
STAT = 144


def attend_kernel(idx, *refs):
    q_refs, kv_ref = refs[0:4], refs[4]
    o_refs = refs[5:7]
    k_s, v_s, qx, s0, s1 = refs[7:]
    scores = (s0, s1)
    f, r = idx[2], idx[3]
    lane = lax.broadcasted_iota(jnp.int32, (32, 128), 1)
    col = lax.broadcasted_iota(jnp.int32, (128, 128), 1)
    row = lax.broadcasted_iota(jnp.int32, (128, 128), 0)
    for p in range(KEYS // 128):
        ks, vs = [], []
        for rr in range(4):
            a = kv_ref[2 * p, rr].astype(F32)
            b = kv_ref[2 * p + 1, rr].astype(F32)
            ks.append(jnp.where(lane < 64, a, pltpu.roll(b, 64, 1)).astype(BF16))
            vs.append(jnp.where(lane < 64, pltpu.roll(a, 64, 1), b).astype(BF16))
        key = jnp.concatenate([x[0:16] for x in ks] + [x[16:32] for x in ks], axis=0)
        k_s[p * 128:(p + 1) * 128, 0:128] = key.T
        blk = 2 * p + row // 64
        extra = jnp.where((blk == f) & (col == row % 64), 1.0, 0.0)
        extra = jnp.where((blk > f) & (col == 64), 1.0, extra)
        k_s[p * 128:(p + 1) * 128, 128:256] = extra.astype(BF16)
        v_s[:, p * 128:(p + 1) * 128] = jnp.concatenate(vs, axis=0)
    t = lax.broadcasted_iota(jnp.int32, (128, 256), 0)
    i = lax.broadcasted_iota(jnp.int32, (128, 256), 1)
    hidden = ((t < 64) & (64 * r + t > i)) | (t == 64)
    qx[...] = jnp.where(hidden, masked_score, 0.0).astype(BF16)

    def queries(h):
        return jnp.concatenate([q_refs[h // 2][h % 2], qx[...]], axis=0)

    def score(h, j, q, top):
        s = jnp.dot(k_s[j * CHUNK:(j + 1) * CHUNK], q, preferred_element_type=F32)
        scores[h % 2][j * CHUNK:(j + 1) * CHUNK] = s
        part = jnp.max(s.reshape(CHUNK // 8, 8, 256), axis=0)
        return part if top is None else jnp.maximum(top, part)

    chunks = KEYS // CHUNK
    tops, q = None, queries(0)
    for j in range(chunks):
        tops = score(0, j, q, tops)
    for h in range(8):
        top = jnp.max(tops, axis=0, keepdims=True)
        tops, acc, total = None, None, None
        if h < 7:
            q = queries(h + 1)
        for j in range(chunks):
            if h < 7:
                tops = score(h + 1, j, q, tops)
            p = jnp.exp2((scores[h % 2][j * CHUNK:(j + 1) * CHUNK] - top) * EXP_SCALE)
            part = jnp.sum(p.reshape(CHUNK // 8, 8, 256), axis=0)
            mix = jnp.dot(
                v_s[:, j * CHUNK:(j + 1) * CHUNK], p.astype(BF16), preferred_element_type=F32
            )
            acc = mix if acc is None else acc + mix
            total = part if total is None else total + part
        total = jnp.sum(total, axis=0, keepdims=True)
        o_ref, at = o_refs[h // 2 % 2], (h // 4 * 2 + h % 2) * STAT
        o_ref[at:at + 128] = (acc / total).astype(BF16)
        put_log(o_ref, at, top * EXP_SCALE + jnp.log2(total))


def attend(idx, qs, kv):
    shape = jax.ShapeDtypeStruct((4 * STAT, 256), BF16)
    return pl.pallas_call(
        attend_kernel,
        in_specs=[sspec()] + [vspec()] * 5,
        out_specs=[vspec()] * 2,
        out_shape=[shape] * 2,
        scratch_shapes=[
            VMEM((KEYS, 256), BF16), VMEM((128, KEYS), BF16), VMEM((128, 256), BF16),
            VMEM((KEYS, 256), F32), VMEM((KEYS, 256), F32),
        ],
        compiler_params=params(),
        cost_estimate=cost(4 * 2048 * 2048 * 128, 4 << 20, 2048 * 2048),
        name="attend",
    )(idx, *qs, kv)


def log_sum(ref, at):
    t = ref[at + 128:at + STAT].astype(F32)
    return t[0:1] + t[1:2] + t[2:3]


def put_log(ref, at, log):
    w = lax.broadcasted_iota(jnp.int32, (16, 256), 0)
    hi = log.astype(BF16).astype(F32)
    mid = (log - hi).astype(BF16).astype(F32)
    terms = jnp.where(w == 0, hi, jnp.where(w == 1, mid, jnp.where(w == 2, log - hi - mid, 0.0)))
    ref[at + 128:at + STAT] = terms.astype(BF16)


def merged(a_ref, b_ref, i, j):
    a, b = log_sum(a_ref, i), log_sum(b_ref, j)
    top = jnp.maximum(a, b)
    fa, fb = jnp.exp2(a - top), jnp.exp2(b - top)
    total = fa + fb
    mixed = a_ref[i:i + 128].astype(F32) * (fa / total)
    mixed = mixed + b_ref[j:j + 128].astype(F32) * (fb / total)
    return mixed, top + jnp.log2(total)


def merge_kernel(a_ref, b_ref, o_ref):
    for h in range(4):
        at = h * STAT
        mixed, log = merged(a_ref, b_ref, at, at)
        o_ref[at:at + 128] = mixed.astype(BF16)
        put_log(o_ref, at, log)


def last_kernel(a_ref, b_ref, out_ref):
    for h in range(4):
        mixed, _ = merged(a_ref, b_ref, h * STAT, (h + 2) % 4 * STAT)
        out_ref[:, h * 128:(h + 1) * 128] = mixed.T.astype(BF16)


def place_kernel(idx, mine_ref, other_ref, out_ref):
    r = idx[3]
    for i in range(2):
        for mask, ref in ((0, mine_ref), (1, other_ref)):
            col = pl.multiple_of(((r ^ mask) ^ (i * 2)) * 256, 256)
            out_ref[:, pl.ds(col, 256)] = ref[:, i * 256:(i + 1) * 256]


def small(kernel, args, shapes, name, scalars=0):
    return pl.pallas_call(
        kernel,
        in_specs=[sspec()] * scalars + [vspec()] * (len(args) - scalars),
        out_specs=[vspec()] * len(shapes),
        out_shape=[jax.ShapeDtypeStruct(shape, BF16) for shape in shapes],
        compiler_params=params(),
        cost_estimate=cost(1 << 19, 1 << 20),
        name=name,
    )(*args)


REP = ("zl", "c")


def to_rep(x, mask):
    if mask == 1:
        return lax.ppermute(x, "c", SWAP)
    if mask == 2:
        return lax.ppermute(x, "zl", SWAP)
    return lax.ppermute(x, REP, [(i, i ^ mask) for i in range(4)])


def average(send, keep, zl, dtype):
    half = keep + lax.ppermute(send, "c", SWAP)
    mine = jnp.where(zl == 0, half[0], half[1])
    theirs = jnp.where(zl == 0, half[1], half[0]).astype(dtype)
    return mine, lax.ppermute(theirs, "zl", SWAP)


def local(tokens, query_ckpt, key_value_ckpt, numerators):
    zl, c, zh = lax.axis_index("zl"), lax.axis_index("c"), lax.axis_index("zh")
    f = lax.axis_index(("zh", "x", "y"))
    r = zl * 2 + c
    idx = jnp.stack([zh, c, f, r, lax.axis_index("x"), lax.axis_index("y")]).astype(jnp.int32)

    send, keep = prepare(idx, numerators, query_ckpt, key_value_ckpt)
    w_mine, w_got = average(send, keep, zl, BF16)

    scale, out = normalise(idx, tokens)
    out, w_got = lax.optimization_barrier((out, w_got))
    w = (w_mine + w_got.astype(F32)).astype(BF16)
    w_all = gather_plane(w)
    got = lax.ppermute(out, "zh", SWAP)
    width = got.shape[1] // 4
    other = [lax.ppermute(got[:, i * width:(i + 1) * width], "c", SWAP) for i in range(4)]

    inverse_freq = jnp.exp(
        -(jnp.arange(64, dtype=F32) * (2.0 / HEAD)) * math.log(theta_base)
    )
    positions = (f * 256 + jnp.arange(256, dtype=jnp.int32)).astype(F32)
    angles = positions[:, None] * inverse_freq[None, :]
    cos, sin = jnp.cos(angles), jnp.sin(angles)
    my_freq = lax.dynamic_slice_in_dim(inverse_freq, r * 16, 16)
    angles_t = positions[None, :] * my_freq[:, None]
    cos_t, sin_t = jnp.cos(angles_t), jnp.sin(angles_t)

    (theirs,) = project(
        theirs_kernel, (idx, *w_all, got, *other), [jax.ShapeDtypeStruct((384, 256), BF16)],
        "theirs", [VMEM((256, 2048), BF16)])
    back = lax.ppermute(theirs, "zh", SWAP)
    q_own, pair_own = project(
        own_kernel, (idx, *w_all, tokens, scale),
        [jax.ShapeDtypeStruct((256, 256), F32), jax.ShapeDtypeStruct((64, 256), F32)], "own")
    pair = finish(
        pair_finish_kernel, (pair_own, back, cos_t, sin_t), (32, 4, 32, 128), "pair_finish")
    pair_all = lax.all_to_all(
        pair.reshape(128, 32, 128), ("zh", "x", "y", "zl", "c"), 0, 0)
    q0 = finish(q_finish_kernel, (q_own, back, cos, sin), (2, 128, 256), "q_finish")
    q1, q2 = to_rep(q0, 1), to_rep(q0, 2)
    qs = [q0, q1, q2, to_rep(q2, 1)]

    kept, sent = attend(idx, qs, pair_all.reshape(32, 4, 32, 128))
    (part,) = small(merge_kernel, (kept, to_rep(sent, 1)), [(4 * STAT, 256)], "merge")
    (mine,) = small(last_kernel, (part, to_rep(part, 2)), [(256, 512)], "last")
    (out,) = small(place_kernel, (idx, mine, to_rep(mine, 1)), [(256, 1024)], "place", 1)
    return out


def solution(mesh):
    grid = Mesh(mesh.devices.reshape(2, 2, 2, 4, 4), ("zl", "c", "zh", "x", "y"))
    fsdp = ("zh", "x", "y")
    in_specs = (P(fsdp, None), P(REP, fsdp, None), P(REP, fsdp, None), P())
    return jax.shard_map(
        local, mesh=grid, in_specs=in_specs, out_specs=P(fsdp, None), check_vma=False
    )
```

```python
import functools
import math

import jax
import jax.numpy as jnp
from jax import lax
from jax.experimental import pallas as pl
from jax.experimental.pallas import tpu as pltpu
from jax.sharding import Mesh, PartitionSpec as P

theta_base = 500000.0
eps_norm = 1e-05
masked_score = -1e30
HEAD = 128
F32 = jnp.float32
BF16 = jnp.bfloat16
VMEM = pltpu.VMEM
SMEM = pltpu.SMEM
NT = (((1,), (1,)), ((), ()))
SWAP = [(0, 1), (1, 0)]


def params(mib=20):
    return pltpu.CompilerParams(vmem_limit_bytes=mib * 1024 * 1024)


def cost(flops, nbytes, trans=0):
    return pl.CostEstimate(flops=flops, bytes_accessed=nbytes, transcendentals=trans)


def vspec():
    return pl.BlockSpec(memory_space=VMEM)


def sspec():
    return pl.BlockSpec(memory_space=SMEM)


def pair_order():
    row = lax.broadcasted_iota(jnp.int32, (256, 256), 0)
    col = lax.broadcasted_iota(jnp.int32, (256, 256), 1)
    r, t = row // 64, row % 64
    key = r * 16 + t + jnp.where(t < 16, 0, 48)
    return jnp.where(col == jnp.where(t < 32, key, r * 32 + t + 96), 1.0, 0.0)


def norm_kernel(idx, x_ref, scale_ref, send_ref):
    zh, c = idx[0], idx[1]
    x = x_ref[...].astype(F32)
    scale = lax.rsqrt(jnp.mean(x * x, axis=-1, keepdims=True) + eps_norm)
    scale_ref[...] = jnp.broadcast_to(scale, scale_ref.shape)
    quarter = send_ref.shape[1]
    start = pl.multiple_of(((1 - zh) * 2 + c) * quarter, quarter)
    send_ref[...] = normed(x_ref, start, quarter, scale)


def normed(x_ref, start, width, scale):
    return (x_ref[:, pl.ds(start, width)].astype(F32) * scale).astype(BF16)


def normalise(idx, tokens):
    rows, width = tokens.shape
    step = 128
    return pl.pallas_call(
        norm_kernel,
        grid=(rows // step,),
        in_specs=[sspec(), pl.BlockSpec((step, width), lambda i: (i, 0))],
        out_specs=[
            pl.BlockSpec((step, 128), lambda i: (i, 0)),
            pl.BlockSpec((step, width // 4), lambda i: (i, 0)),
        ],
        out_shape=[
            jax.ShapeDtypeStruct((rows, 128), F32),
            jax.ShapeDtypeStruct((rows, width // 4), BF16),
        ],
        compiler_params=params(),
        cost_estimate=cost(rows * width * 4, rows * width * 3),
        name="normalise",
    )(idx, tokens)


def share_of(idx, num, shape):
    r = idx[3]
    total = num[0] + num[1] + num[2] + num[3]
    mine = jnp.full(shape, num[r], jnp.int32).astype(F32)
    return mine / jnp.full(shape, total, jnp.int32).astype(F32)


def prep_kernel(idx, num, q_ref, kv_ref, send_ref, keep_ref):
    c = idx[1]
    s = share_of(idx, num, (1, 256))
    kvt = lax.dot_general(
        pair_order(), kv_ref[0] * s, NT, precision=lax.Precision.HIGHEST,
        preferred_element_type=F32,
    )
    for zl in range(2):
        keep = pl.multiple_of((zl * 2 + c) * 256, 256)
        send = pl.multiple_of((zl * 2 + 1 - c) * 256, 256)
        first, second = kvt[zl * 128:zl * 128 + 64], kvt[zl * 128 + 64:zl * 128 + 128]
        for ref, col, pair in (
            (keep_ref, keep, jnp.where(c == 0, first, second)),
            (send_ref, send, jnp.where(c == 0, second, first)),
        ):
            for half in range(2):
                at = half * 160
                ref[zl, at:at + 128] = q_ref[0, half * 128:half * 128 + 128, pl.ds(col, 256)] * s
                ref[zl, at + 128:at + 160] = pair[half * 32:half * 32 + 32]


def prepare(idx, num, q, kv):
    shape = jax.ShapeDtypeStruct((2, 320, 256), F32)
    return pl.pallas_call(
        prep_kernel,
        in_specs=[sspec(), sspec()] + [vspec()] * 2,
        out_specs=[vspec(), vspec()],
        out_shape=[shape, shape],
        compiler_params=params(),
        cost_estimate=cost(1 << 20, 3 << 20),
        name="prepare",
    )(idx, num, q, kv)


def ring(step):
    return [(i, (i + step) % 4) for i in range(4)]


def gather_plane(w):
    lower, upper = w[0:160], w[160:320]
    lower = jnp.stack([lower] + [lax.ppermute(lower, "y", ring(d)) for d in (1, 3, 2)])
    upper = jnp.stack([upper] + [lax.ppermute(upper, "x", ring(d)) for d in (1, 3, 2)])
    lower, upper = lax.optimization_barrier((lower, upper))
    lowers = [lower] + [lax.ppermute(lower, "x", ring(d)) for d in (1, 3, 2)]
    uppers = [upper] + [lax.ppermute(upper, "y", ring(d)) for d in (1, 3, 2)]
    return lowers + uppers


def plane_block(idx, w_refs, j):
    back = (0, 1, 3, 2)
    dx, dy = j // 4, j % 4
    low, up = w_refs[dx], w_refs[4 + dy]
    q = jnp.concatenate([low[dy, 0:128], up[dx, 0:128]], axis=0)
    pair = jnp.concatenate([low[dy, 128:160], up[dx, 128:160]], axis=0)
    return q, pair, ((idx[4] + 4 - back[dx]) % 4) * 4 + (idx[5] + 4 - back[dy]) % 4


def accumulate(idx, w_refs, block):
    acc, pair_acc = None, None
    for j in range(16):
        w, pair, at = plane_block(idx, w_refs, j)
        x = block(at)
        part = jnp.dot(x, w, preferred_element_type=F32)
        pair_part = lax.dot_general(x, pair, NT, preferred_element_type=F32)
        acc = part if acc is None else acc + part
        pair_acc = pair_part if pair_acc is None else pair_acc + pair_part
    row = lax.broadcasted_iota(jnp.int32, (64, 64), 0)
    col = lax.broadcasted_iota(jnp.int32, (64, 64), 1)
    pair_acc = lax.dot_general(
        jnp.where(row == col, 1.0, 0.0), pair_acc, NT, precision=lax.Precision.HIGHEST,
        preferred_element_type=F32,
    )
    return acc, pair_acc


def own_kernel(idx, *refs):
    w_refs, (x_ref, scale_ref, q_ref, pair_ref) = refs[:-4], refs[-4:]
    scale = scale_ref[:, 0:1]

    def block(at):
        return normed(x_ref, pl.multiple_of((idx[0] * 16 + at) * 256, 256), 256, scale)

    q_ref[...], pair_ref[...] = accumulate(idx, w_refs, block)


def theirs_kernel(idx, *refs):
    w_refs, xa_ref, xb_refs, (out_ref, xb_ref) = refs[:8], refs[8], refs[9:-2], refs[-2:]
    width = xb_refs[0].shape[1]
    for i, ref in enumerate(xb_refs):
        xb_ref[:, i * width:(i + 1) * width] = ref[...]

    def block(at):
        cols = pl.ds(pl.multiple_of((at % 8) * 256, 256), 256)
        return jnp.where(at // 8 == idx[1], xa_ref[:, cols], xb_ref[:, cols])

    q, pair = accumulate(idx, w_refs, block)
    out_ref[0:256] = q.astype(BF16)
    out_ref[256:320] = pair.astype(BF16)


def project(kernel, args, outs, name, scratch=()):
    return pl.pallas_call(
        kernel,
        scratch_shapes=scratch,
        in_specs=[sspec()] + [vspec()] * (len(args) - 1),
        out_specs=[vspec()] * len(outs),
        out_shape=outs,
        compiler_params=params(),
        cost_estimate=cost(2 * 256 * 320 * 4096, 5 << 20),
        name=name,
    )(*args)


def pair_finish_kernel(own_ref, got_ref, cos_ref, sin_ref, out_ref):
    t = own_ref[...] + got_ref[256:320].astype(F32)
    u, w = t[0:16], t[16:32]
    cos, sin = cos_ref[...], sin_ref[...]
    key = jnp.concatenate([u * cos - w * sin, w * cos + u * sin], axis=0)
    val = t[32:64]
    for r in range(4):
        cols = slice(r * 64, (r + 1) * 64)
        piece = jnp.concatenate([key[:, cols], val[:, cols]], axis=1).astype(BF16)
        for f in range(out_ref.shape[0]):
            out_ref[f, r] = piece


def q_finish_kernel(own_ref, got_ref, cos_ref, sin_ref, out_ref):
    t = own_ref[...] + got_ref[0:256].astype(F32)
    cos, sin = cos_ref[...], sin_ref[...]
    for h in range(2):
        u = t[:, h * 128:h * 128 + 64]
        w = t[:, h * 128 + 64:h * 128 + 128]
        rotated = jnp.concatenate([u * cos - w * sin, w * cos + u * sin], axis=1)
        out_ref[h] = rotated.T.astype(BF16)


def finish(kernel, args, shape, name):
    return pl.pallas_call(
        kernel,
        in_specs=[vspec()] * 4,
        out_specs=vspec(),
        out_shape=jax.ShapeDtypeStruct(shape, BF16),
        compiler_params=params(),
        cost_estimate=cost(1 << 18, 1 << 20),
        name=name,
    )(*args)


CHUNK = 512
KEYS = 2048
EXP_SCALE = math.log2(math.e) / math.sqrt(HEAD)
STATS, ROWS = 512, 528


def attend_kernel(idx, *refs):
    q_refs, kv_ref = refs[0:4], refs[4]
    o_refs = refs[5:7]
    k_s, v_s, qx, s0, s1 = refs[7:]
    scores = (s0, s1)
    f, r = idx[2], idx[3]
    lane = lax.broadcasted_iota(jnp.int32, (32, 128), 1)
    col = lax.broadcasted_iota(jnp.int32, (128, 128), 1)
    row = lax.broadcasted_iota(jnp.int32, (128, 128), 0)
    for p in range(KEYS // 128):
        ks, vs = [], []
        for rr in range(4):
            a = kv_ref[2 * p, rr].astype(F32)
            b = kv_ref[2 * p + 1, rr].astype(F32)
            ks.append(jnp.where(lane < 64, a, pltpu.roll(b, 64, 1)).astype(BF16))
            vs.append(jnp.where(lane < 64, pltpu.roll(a, 64, 1), b).astype(BF16))
        key = jnp.concatenate([x[0:16] for x in ks] + [x[16:32] for x in ks], axis=0)
        k_s[p * 128:(p + 1) * 128, 0:128] = key.T
        blk = 2 * p + row // 64
        extra = jnp.where((blk == f) & (col == row % 64), 1.0, 0.0)
        extra = jnp.where((blk > f) & (col == 64), 1.0, extra)
        k_s[p * 128:(p + 1) * 128, 128:256] = extra.astype(BF16)
        v_s[:, p * 128:(p + 1) * 128] = jnp.concatenate(vs, axis=0)
    t = lax.broadcasted_iota(jnp.int32, (128, 256), 0)
    i = lax.broadcasted_iota(jnp.int32, (128, 256), 1)
    hidden = ((t < 64) & (64 * r + t > i)) | (t == 64)
    qx[...] = jnp.where(hidden, masked_score, 0.0).astype(BF16)

    def queries(h):
        return jnp.concatenate([q_refs[h // 2][h % 2], qx[...]], axis=0)

    def score(h, j, q, top):
        s = jnp.dot(k_s[j * CHUNK:(j + 1) * CHUNK], q, preferred_element_type=F32)
        scores[h % 2][j * CHUNK:(j + 1) * CHUNK] = s
        part = jnp.max(s.reshape(CHUNK // 8, 8, 256), axis=0)
        return part if top is None else jnp.maximum(top, part)

    chunks = KEYS // CHUNK
    tops, q = None, queries(0)
    for j in range(chunks):
        tops = score(0, j, q, tops)
    logs = ([], [])
    for h in range(8):
        top = jnp.max(tops, axis=0, keepdims=True)
        tops, acc, total = None, None, None
        if h < 7:
            q = queries(h + 1)
        for j in range(chunks):
            if h < 7:
                tops = score(h + 1, j, q, tops)
            p = jnp.exp2((scores[h % 2][j * CHUNK:(j + 1) * CHUNK] - top) * EXP_SCALE)
            part = jnp.sum(p.reshape(CHUNK // 8, 8, 256), axis=0)
            mix = jnp.dot(
                v_s[:, j * CHUNK:(j + 1) * CHUNK], p.astype(BF16), preferred_element_type=F32
            )
            acc = mix if acc is None else acc + mix
            total = part if total is None else total + part
        total = jnp.sum(total, axis=0, keepdims=True)
        to, at = h // 2 % 2, (h // 4 * 2 + h % 2) * 128
        o_refs[to][at:at + 128] = (acc / total).astype(BF16)
        logs[to].append(top * EXP_SCALE + jnp.log2(total))
    for o_ref, log in zip(o_refs, logs):
        put_logs(o_ref, log)


def attend(idx, qs, kv):
    shape = jax.ShapeDtypeStruct((ROWS, 256), BF16)
    return pl.pallas_call(
        attend_kernel,
        in_specs=[sspec()] + [vspec()] * 5,
        out_specs=[vspec()] * 2,
        out_shape=[shape] * 2,
        scratch_shapes=[
            VMEM((KEYS, 256), BF16), VMEM((128, KEYS), BF16), VMEM((128, 256), BF16),
            VMEM((KEYS, 256), F32), VMEM((KEYS, 256), F32),
        ],
        compiler_params=params(),
        cost_estimate=cost(4 * 2048 * 2048 * 128, 4 << 20, 2048 * 2048),
        name="attend",
    )(idx, *qs, kv)


def log_sum(ref, h):
    t = ref[STATS:ROWS].astype(F32)
    return t[3 * h:3 * h + 1] + t[3 * h + 1:3 * h + 2] + t[3 * h + 2:3 * h + 3]


def put_logs(ref, logs):
    w = lax.broadcasted_iota(jnp.int32, (ROWS - STATS, 256), 0)
    terms = jnp.zeros(w.shape, F32)
    for h, log in enumerate(logs):
        hi = log.astype(BF16).astype(F32)
        mid = (log - hi).astype(BF16).astype(F32)
        for k, term in enumerate((hi, mid, log - hi - mid)):
            terms = jnp.where(w == 3 * h + k, term, terms)
    ref[STATS:ROWS] = terms.astype(BF16)


def merged(a_ref, b_ref, i, j):
    a, b = log_sum(a_ref, i), log_sum(b_ref, j)
    top = jnp.maximum(a, b)
    fa, fb = jnp.exp2(a - top), jnp.exp2(b - top)
    total = fa + fb
    mixed = a_ref[i * 128:i * 128 + 128].astype(F32) * (fa / total)
    mixed = mixed + b_ref[j * 128:j * 128 + 128].astype(F32) * (fb / total)
    return mixed, top + jnp.log2(total)


def merge_kernel(a_ref, b_ref, o_ref):
    logs = []
    for h in range(4):
        mixed, log = merged(a_ref, b_ref, h, h)
        o_ref[h * 128:h * 128 + 128] = mixed.astype(BF16)
        logs.append(log)
    put_logs(o_ref, logs)


def last_kernel(a_ref, b_ref, out_ref):
    for h in range(4):
        mixed, _ = merged(a_ref, b_ref, h, (h + 2) % 4)
        out_ref[:, h * 128:(h + 1) * 128] = mixed.T.astype(BF16)


def place_kernel(idx, mine_ref, other_ref, out_ref):
    r = idx[3]
    for i in range(2):
        for mask, ref in ((0, mine_ref), (1, other_ref)):
            col = pl.multiple_of(((r ^ mask) ^ (i * 2)) * 256, 256)
            out_ref[:, pl.ds(col, 256)] = ref[:, i * 256:(i + 1) * 256]


def small(kernel, args, shapes, name, scalars=0):
    return pl.pallas_call(
        kernel,
        in_specs=[sspec()] * scalars + [vspec()] * (len(args) - scalars),
        out_specs=[vspec()] * len(shapes),
        out_shape=[jax.ShapeDtypeStruct(shape, BF16) for shape in shapes],
        compiler_params=params(),
        cost_estimate=cost(1 << 19, 1 << 20),
        name=name,
    )(*args)


REP = ("zl", "c")


def to_rep(x, mask):
    if mask == 1:
        return lax.ppermute(x, "c", SWAP)
    if mask == 2:
        return lax.ppermute(x, "zl", SWAP)
    return lax.ppermute(x, REP, [(i, i ^ mask) for i in range(4)])


def average(send, keep, zl, dtype):
    half = keep + lax.ppermute(send, "c", SWAP)
    mine = jnp.where(zl == 0, half[0], half[1])
    theirs = jnp.where(zl == 0, half[1], half[0]).astype(dtype)
    return mine, lax.ppermute(theirs, "zl", SWAP)


def local(tokens, query_ckpt, key_value_ckpt, numerators):
    zl, c, zh = lax.axis_index("zl"), lax.axis_index("c"), lax.axis_index("zh")
    f = lax.axis_index(("zh", "x", "y"))
    r = zl * 2 + c
    idx = jnp.stack([zh, c, f, r, lax.axis_index("x"), lax.axis_index("y")]).astype(jnp.int32)

    send, keep = prepare(idx, numerators, query_ckpt, key_value_ckpt)
    w_mine, w_got = average(send, keep, zl, BF16)

    scale, out = normalise(idx, tokens)
    out, w_got = lax.optimization_barrier((out, w_got))
    w = (w_mine + w_got.astype(F32)).astype(BF16)
    w_all = gather_plane(w)
    got = lax.ppermute(out, "zh", SWAP)
    width = got.shape[1] // 4
    other = [lax.ppermute(got[:, i * width:(i + 1) * width], "c", SWAP) for i in range(4)]

    inverse_freq = jnp.exp(
        -(jnp.arange(64, dtype=F32) * (2.0 / HEAD)) * math.log(theta_base)
    )
    positions = (f * 256 + jnp.arange(256, dtype=jnp.int32)).astype(F32)
    angles = positions[:, None] * inverse_freq[None, :]
    cos, sin = jnp.cos(angles), jnp.sin(angles)
    my_freq = lax.dynamic_slice_in_dim(inverse_freq, r * 16, 16)
    angles_t = positions[None, :] * my_freq[:, None]
    cos_t, sin_t = jnp.cos(angles_t), jnp.sin(angles_t)

    (theirs,) = project(
        theirs_kernel, (idx, *w_all, got, *other), [jax.ShapeDtypeStruct((320, 256), BF16)],
        "theirs", [VMEM((256, 2048), BF16)])
    back = lax.ppermute(theirs, "zh", SWAP)
    q_own, pair_own = project(
        own_kernel, (idx, *w_all, tokens, scale),
        [jax.ShapeDtypeStruct((256, 256), F32), jax.ShapeDtypeStruct((64, 256), F32)], "own")
    pair = finish(
        pair_finish_kernel, (pair_own, back, cos_t, sin_t), (32, 4, 32, 128), "pair_finish")
    pair_all = lax.all_to_all(
        pair.reshape(128, 32, 128), ("zh", "x", "y", "zl", "c"), 0, 0)
    q0 = finish(q_finish_kernel, (q_own, back, cos, sin), (2, 128, 256), "q_finish")
    q1, q2 = to_rep(q0, 1), to_rep(q0, 2)
    qs = [q0, q1, q2, to_rep(q2, 1)]

    kept, sent = attend(idx, qs, pair_all.reshape(32, 4, 32, 128))
    (part,) = small(merge_kernel, (kept, to_rep(sent, 1)), [(ROWS, 256)], "merge")
    (mine,) = small(last_kernel, (part, to_rep(part, 2)), [(256, 512)], "last")
    (out,) = small(place_kernel, (idx, mine, to_rep(mine, 1)), [(256, 1024)], "place", 1)
    return out


def solution(mesh):
    grid = Mesh(mesh.devices.reshape(2, 2, 2, 4, 4), ("zl", "c", "zh", "x", "y"))
    fsdp = ("zh", "x", "y")
    in_specs = (P(fsdp, None), P(REP, fsdp, None), P(REP, fsdp, None), P())
    return jax.shard_map(
        local, mesh=grid, in_specs=in_specs, out_specs=P(fsdp, None), check_vma=False
    )
```

```python
import functools
import math

import jax
import jax.numpy as jnp
from jax import lax
from jax.experimental import pallas as pl
from jax.experimental.pallas import tpu as pltpu
from jax.sharding import Mesh, PartitionSpec as P

theta_base = 500000.0
eps_norm = 1e-05
masked_score = -1e30
HEAD = 128
F32 = jnp.float32
BF16 = jnp.bfloat16
VMEM = pltpu.VMEM
SMEM = pltpu.SMEM
NT = (((1,), (1,)), ((), ()))
SWAP = [(0, 1), (1, 0)]


def params(mib=20):
    return pltpu.CompilerParams(vmem_limit_bytes=mib * 1024 * 1024)


def cost(flops, nbytes, trans=0):
    return pl.CostEstimate(flops=flops, bytes_accessed=nbytes, transcendentals=trans)


def vspec():
    return pl.BlockSpec(memory_space=VMEM)


def sspec():
    return pl.BlockSpec(memory_space=SMEM)


def pair_order():
    row = lax.broadcasted_iota(jnp.int32, (256, 256), 0)
    col = lax.broadcasted_iota(jnp.int32, (256, 256), 1)
    r, t = row // 64, row % 64
    key = r * 16 + t + jnp.where(t < 16, 0, 48)
    return jnp.where(col == jnp.where(t < 32, key, r * 32 + t + 96), 1.0, 0.0)


def norm_kernel(idx, x_ref, scale_ref, send_ref):
    zh, c = idx[0], idx[1]
    x = x_ref[...].astype(F32)
    scale = lax.rsqrt(jnp.mean(x * x, axis=-1, keepdims=True) + eps_norm)
    scale_ref[...] = jnp.broadcast_to(scale, scale_ref.shape)
    quarter = send_ref.shape[1]
    start = pl.multiple_of(((1 - zh) * 2 + c) * quarter, quarter)
    send_ref[...] = normed(x_ref, start, quarter, scale)


def normed(x_ref, start, width, scale):
    return (x_ref[:, pl.ds(start, width)].astype(F32) * scale).astype(BF16)


def normalise(idx, tokens):
    rows, width = tokens.shape
    step = 128
    return pl.pallas_call(
        norm_kernel,
        grid=(rows // step,),
        in_specs=[sspec(), pl.BlockSpec((step, width), lambda i: (i, 0))],
        out_specs=[
            pl.BlockSpec((step, 128), lambda i: (i, 0)),
            pl.BlockSpec((step, width // 4), lambda i: (i, 0)),
        ],
        out_shape=[
            jax.ShapeDtypeStruct((rows, 128), F32),
            jax.ShapeDtypeStruct((rows, width // 4), BF16),
        ],
        compiler_params=params(),
        cost_estimate=cost(rows * width * 4, rows * width * 3),
        name="normalise",
    )(idx, tokens)


def share_of(idx, num, shape):
    r = idx[3]
    total = num[0] + num[1] + num[2] + num[3]
    mine = jnp.full(shape, num[r], jnp.int32).astype(F32)
    return mine / jnp.full(shape, total, jnp.int32).astype(F32)


def prep_kernel(idx, num, q_ref, kv_ref, send_ref, keep_ref):
    c = idx[1]
    s = share_of(idx, num, (1, 256))
    kvt = lax.dot_general(
        pair_order(), kv_ref[0] * s, NT, precision=lax.Precision.HIGHEST,
        preferred_element_type=F32,
    )
    for zl in range(2):
        keep = pl.multiple_of((zl * 2 + c) * 256, 256)
        send = pl.multiple_of((zl * 2 + 1 - c) * 256, 256)
        first, second = kvt[zl * 128:zl * 128 + 64], kvt[zl * 128 + 64:zl * 128 + 128]
        for ref, col, pair in (
            (keep_ref, keep, jnp.where(c == 0, first, second)),
            (send_ref, send, jnp.where(c == 0, second, first)),
        ):
            for half in range(2):
                at = half * 160
                ref[zl, at:at + 128] = (q_ref[0, half * 128:half * 128 + 128, pl.ds(col, 256)] * s).astype(ref.dtype)
                ref[zl, at + 128:at + 160] = pair[half * 32:half * 32 + 32].astype(ref.dtype)


def prepare(idx, num, q, kv):
    shape = jax.ShapeDtypeStruct((2, 320, 256), F32)
    return pl.pallas_call(
        prep_kernel,
        in_specs=[sspec(), sspec()] + [vspec()] * 2,
        out_specs=[vspec(), vspec()],
        out_shape=[jax.ShapeDtypeStruct(shape.shape, BF16), shape],
        compiler_params=params(),
        cost_estimate=cost(1 << 20, 3 << 20),
        name="prepare",
    )(idx, num, q, kv)


def ring(step):
    return [(i, (i + step) % 4) for i in range(4)]


def gather_plane(w):
    lower, upper = w[0:160], w[160:320]
    lower = jnp.stack([lower] + [lax.ppermute(lower, "y", ring(d)) for d in (1, 3, 2)])
    upper = jnp.stack([upper] + [lax.ppermute(upper, "x", ring(d)) for d in (1, 3, 2)])
    lower, upper = lax.optimization_barrier((lower, upper))
    lowers = [lower] + [lax.ppermute(lower, "x", ring(d)) for d in (1, 3, 2)]
    uppers = [upper] + [lax.ppermute(upper, "y", ring(d)) for d in (1, 3, 2)]
    return lowers + uppers


def plane_block(idx, w_refs, j):
    back = (0, 1, 3, 2)
    dx, dy = j // 4, j % 4
    low, up = w_refs[dx], w_refs[4 + dy]
    q = jnp.concatenate([low[dy, 0:128], up[dx, 0:128]], axis=0)
    pair = jnp.concatenate([low[dy, 128:160], up[dx, 128:160]], axis=0)
    return q, pair, ((idx[4] + 4 - back[dx]) % 4) * 4 + (idx[5] + 4 - back[dy]) % 4


def accumulate(idx, w_refs, block):
    acc, pair_acc = None, None
    for j in range(16):
        w, pair, at = plane_block(idx, w_refs, j)
        x = block(at)
        part = jnp.dot(x, w, preferred_element_type=F32)
        pair_part = lax.dot_general(x, pair, NT, preferred_element_type=F32)
        acc = part if acc is None else acc + part
        pair_acc = pair_part if pair_acc is None else pair_acc + pair_part
    row = lax.broadcasted_iota(jnp.int32, (64, 64), 0)
    col = lax.broadcasted_iota(jnp.int32, (64, 64), 1)
    pair_acc = lax.dot_general(
        jnp.where(row == col, 1.0, 0.0), pair_acc, NT, precision=lax.Precision.HIGHEST,
        preferred_element_type=F32,
    )
    return acc, pair_acc


def own_kernel(idx, *refs):
    w_refs, (x_ref, scale_ref, q_ref, pair_ref) = refs[:-4], refs[-4:]
    scale = scale_ref[:, 0:1]

    def block(at):
        return normed(x_ref, pl.multiple_of((idx[0] * 16 + at) * 256, 256), 256, scale)

    q_ref[...], pair_ref[...] = accumulate(idx, w_refs, block)


def theirs_kernel(idx, *refs):
    w_refs, xa_ref, xb_refs, (out_ref, xb_ref) = refs[:8], refs[8], refs[9:-2], refs[-2:]
    width = xb_refs[0].shape[1]
    for i, ref in enumerate(xb_refs):
        xb_ref[:, i * width:(i + 1) * width] = ref[...]

    def block(at):
        cols = pl.ds(pl.multiple_of((at % 8) * 256, 256), 256)
        return jnp.where(at // 8 == idx[1], xa_ref[:, cols], xb_ref[:, cols])

    q, pair = accumulate(idx, w_refs, block)
    out_ref[0:256] = q.astype(BF16)
    out_ref[256:320] = pair.astype(BF16)


def project(kernel, args, outs, name, scratch=()):
    return pl.pallas_call(
        kernel,
        scratch_shapes=scratch,
        in_specs=[sspec()] + [vspec()] * (len(args) - 1),
        out_specs=[vspec()] * len(outs),
        out_shape=outs,
        compiler_params=params(),
        cost_estimate=cost(2 * 256 * 320 * 4096, 5 << 20),
        name=name,
    )(*args)


def pair_finish_kernel(own_ref, got_ref, cos_ref, sin_ref, out_ref):
    t = own_ref[...] + got_ref[256:320].astype(F32)
    u, w = t[0:16], t[16:32]
    cos, sin = cos_ref[...], sin_ref[...]
    key = jnp.concatenate([u * cos - w * sin, w * cos + u * sin], axis=0)
    val = t[32:64]
    for r in range(4):
        cols = slice(r * 64, (r + 1) * 64)
        piece = jnp.concatenate([key[:, cols], val[:, cols]], axis=1).astype(BF16)
        for f in range(out_ref.shape[0]):
            out_ref[f, r] = piece


def q_finish_kernel(own_ref, got_ref, cos_ref, sin_ref, out_ref):
    t = own_ref[...] + got_ref[0:256].astype(F32)
    cos, sin = cos_ref[...], sin_ref[...]
    for h in range(2):
        u = t[:, h * 128:h * 128 + 64]
        w = t[:, h * 128 + 64:h * 128 + 128]
        rotated = jnp.concatenate([u * cos - w * sin, w * cos + u * sin], axis=1)
        out_ref[h] = rotated.T.astype(BF16)


def finish(kernel, args, shape, name):
    return pl.pallas_call(
        kernel,
        in_specs=[vspec()] * 4,
        out_specs=vspec(),
        out_shape=jax.ShapeDtypeStruct(shape, BF16),
        compiler_params=params(),
        cost_estimate=cost(1 << 18, 1 << 20),
        name=name,
    )(*args)


CHUNK = 512
KEYS = 2048
EXP_SCALE = math.log2(math.e) / math.sqrt(HEAD)
STATS, ROWS = 512, 528


def attend_kernel(idx, *refs):
    q_refs, kv_ref = refs[0:4], refs[4]
    o_refs = refs[5:7]
    k_s, v_s, qx, s0, s1 = refs[7:]
    scores = (s0, s1)
    f, r = idx[2], idx[3]
    lane = lax.broadcasted_iota(jnp.int32, (32, 128), 1)
    col = lax.broadcasted_iota(jnp.int32, (128, 128), 1)
    row = lax.broadcasted_iota(jnp.int32, (128, 128), 0)
    for p in range(KEYS // 128):
        ks, vs = [], []
        for rr in range(4):
            a = kv_ref[2 * p, rr].astype(F32)
            b = kv_ref[2 * p + 1, rr].astype(F32)
            ks.append(jnp.where(lane < 64, a, pltpu.roll(b, 64, 1)).astype(BF16))
            vs.append(jnp.where(lane < 64, pltpu.roll(a, 64, 1), b).astype(BF16))
        key = jnp.concatenate([x[0:16] for x in ks] + [x[16:32] for x in ks], axis=0)
        k_s[p * 128:(p + 1) * 128, 0:128] = key.T
        blk = 2 * p + row // 64
        extra = jnp.where((blk == f) & (col == row % 64), 1.0, 0.0)
        extra = jnp.where((blk > f) & (col == 64), 1.0, extra)
        k_s[p * 128:(p + 1) * 128, 128:256] = extra.astype(BF16)
        v_s[:, p * 128:(p + 1) * 128] = jnp.concatenate(vs, axis=0)
    t = lax.broadcasted_iota(jnp.int32, (128, 256), 0)
    i = lax.broadcasted_iota(jnp.int32, (128, 256), 1)
    hidden = ((t < 64) & (64 * r + t > i)) | (t == 64)
    qx[...] = jnp.where(hidden, masked_score, 0.0).astype(BF16)

    def queries(h):
        return jnp.concatenate([q_refs[h // 2][h % 2], qx[...]], axis=0)

    def score(h, j, q, top):
        s = jnp.dot(k_s[j * CHUNK:(j + 1) * CHUNK], q, preferred_element_type=F32)
        scores[h % 2][j * CHUNK:(j + 1) * CHUNK] = s
        part = jnp.max(s.reshape(CHUNK // 8, 8, 256), axis=0)
        return part if top is None else jnp.maximum(top, part)

    chunks = KEYS // CHUNK
    tops, q = None, queries(0)
    for j in range(chunks):
        tops = score(0, j, q, tops)
    logs = ([], [])
    for h in range(8):
        top = jnp.max(tops, axis=0, keepdims=True)
        tops, acc, total = None, None, None
        if h < 7:
            q = queries(h + 1)
        for j in range(chunks):
            if h < 7:
                tops = score(h + 1, j, q, tops)
            p = jnp.exp2((scores[h % 2][j * CHUNK:(j + 1) * CHUNK] - top) * EXP_SCALE)
            part = jnp.sum(p.reshape(CHUNK // 8, 8, 256), axis=0)
            mix = jnp.dot(
                v_s[:, j * CHUNK:(j + 1) * CHUNK], p.astype(BF16), preferred_element_type=F32
            )
            acc = mix if acc is None else acc + mix
            total = part if total is None else total + part
        total = jnp.sum(total, axis=0, keepdims=True)
        to, at = h // 2 % 2, (h // 4 * 2 + h % 2) * 128
        o_refs[to][at:at + 128] = (acc / total).astype(BF16)
        logs[to].append(top * EXP_SCALE + jnp.log2(total))
    for o_ref, log in zip(o_refs, logs):
        put_logs(o_ref, log)


def attend(idx, qs, kv):
    shape = jax.ShapeDtypeStruct((ROWS, 256), BF16)
    return pl.pallas_call(
        attend_kernel,
        in_specs=[sspec()] + [vspec()] * 5,
        out_specs=[vspec()] * 2,
        out_shape=[shape] * 2,
        scratch_shapes=[
            VMEM((KEYS, 256), BF16), VMEM((128, KEYS), BF16), VMEM((128, 256), BF16),
            VMEM((KEYS, 256), F32), VMEM((KEYS, 256), F32),
        ],
        compiler_params=params(),
        cost_estimate=cost(4 * 2048 * 2048 * 128, 4 << 20, 2048 * 2048),
        name="attend",
    )(idx, *qs, kv)


def log_sum(ref, h):
    t = ref[STATS:ROWS].astype(F32)
    return t[3 * h:3 * h + 1] + t[3 * h + 1:3 * h + 2] + t[3 * h + 2:3 * h + 3]


def put_logs(ref, logs):
    w = lax.broadcasted_iota(jnp.int32, (ROWS - STATS, 256), 0)
    terms = jnp.zeros(w.shape, F32)
    for h, log in enumerate(logs):
        hi = log.astype(BF16).astype(F32)
        mid = (log - hi).astype(BF16).astype(F32)
        for k, term in enumerate((hi, mid, log - hi - mid)):
            terms = jnp.where(w == 3 * h + k, term, terms)
    ref[STATS:ROWS] = terms.astype(BF16)


def merged(a_ref, b_ref, i, j):
    a, b = log_sum(a_ref, i), log_sum(b_ref, j)
    top = jnp.maximum(a, b)
    fa, fb = jnp.exp2(a - top), jnp.exp2(b - top)
    total = fa + fb
    mixed = a_ref[i * 128:i * 128 + 128].astype(F32) * (fa / total)
    mixed = mixed + b_ref[j * 128:j * 128 + 128].astype(F32) * (fb / total)
    return mixed, top + jnp.log2(total)


def merge_kernel(a_ref, b_ref, o_ref):
    logs = []
    for h in range(4):
        mixed, log = merged(a_ref, b_ref, h, h)
        o_ref[h * 128:h * 128 + 128] = mixed.astype(BF16)
        logs.append(log)
    put_logs(o_ref, logs)


def last_kernel(a_ref, b_ref, out_ref):
    for h in range(4):
        mixed, _ = merged(a_ref, b_ref, h, (h + 2) % 4)
        out_ref[:, h * 128:(h + 1) * 128] = mixed.T.astype(BF16)


def place_kernel(idx, mine_ref, other_ref, out_ref):
    r = idx[3]
    for i in range(2):
        for mask, ref in ((0, mine_ref), (1, other_ref)):
            col = pl.multiple_of(((r ^ mask) ^ (i * 2)) * 256, 256)
            out_ref[:, pl.ds(col, 256)] = ref[:, i * 256:(i + 1) * 256]


def small(kernel, args, shapes, name, scalars=0):
    return pl.pallas_call(
        kernel,
        in_specs=[sspec()] * scalars + [vspec()] * (len(args) - scalars),
        out_specs=[vspec()] * len(shapes),
        out_shape=[jax.ShapeDtypeStruct(shape, BF16) for shape in shapes],
        compiler_params=params(),
        cost_estimate=cost(1 << 19, 1 << 20),
        name=name,
    )(*args)


REP = ("zl", "c")


def to_rep(x, mask):
    if mask == 1:
        return lax.ppermute(x, "c", SWAP)
    if mask == 2:
        return lax.ppermute(x, "zl", SWAP)
    return lax.ppermute(x, REP, [(i, i ^ mask) for i in range(4)])


def average(send, keep, zl, dtype):
    half = keep + lax.ppermute(send, "c", SWAP).astype(F32)
    mine = jnp.where(zl == 0, half[0], half[1])
    theirs = jnp.where(zl == 0, half[1], half[0]).astype(dtype)
    return mine, lax.ppermute(theirs, "zl", SWAP)


def local(tokens, query_ckpt, key_value_ckpt, numerators):
    zl, c, zh = lax.axis_index("zl"), lax.axis_index("c"), lax.axis_index("zh")
    f = lax.axis_index(("zh", "x", "y"))
    r = zl * 2 + c
    idx = jnp.stack([zh, c, f, r, lax.axis_index("x"), lax.axis_index("y")]).astype(jnp.int32)

    send, keep = prepare(idx, numerators, query_ckpt, key_value_ckpt)
    w_mine, w_got = average(send, keep, zl, BF16)

    scale, out = normalise(idx, tokens)
    out, w_got = lax.optimization_barrier((out, w_got))
    w = (w_mine + w_got.astype(F32)).astype(BF16)
    w_all = gather_plane(w)
    got = lax.ppermute(out, "zh", SWAP)
    width = got.shape[1] // 4
    other = [lax.ppermute(got[:, i * width:(i + 1) * width], "c", SWAP) for i in range(4)]

    inverse_freq = jnp.exp(
        -(jnp.arange(64, dtype=F32) * (2.0 / HEAD)) * math.log(theta_base)
    )
    positions = (f * 256 + jnp.arange(256, dtype=jnp.int32)).astype(F32)
    angles = positions[:, None] * inverse_freq[None, :]
    cos, sin = jnp.cos(angles), jnp.sin(angles)
    my_freq = lax.dynamic_slice_in_dim(inverse_freq, r * 16, 16)
    angles_t = positions[None, :] * my_freq[:, None]
    cos_t, sin_t = jnp.cos(angles_t), jnp.sin(angles_t)

    (theirs,) = project(
        theirs_kernel, (idx, *w_all, got, *other), [jax.ShapeDtypeStruct((320, 256), BF16)],
        "theirs", [VMEM((256, 2048), BF16)])
    back = lax.ppermute(theirs, "zh", SWAP)
    q_own, pair_own = project(
        own_kernel, (idx, *w_all, tokens, scale),
        [jax.ShapeDtypeStruct((256, 256), F32), jax.ShapeDtypeStruct((64, 256), F32)], "own")
    pair = finish(
        pair_finish_kernel, (pair_own, back, cos_t, sin_t), (32, 4, 32, 128), "pair_finish")
    pair_all = lax.all_to_all(
        pair.reshape(128, 32, 128), ("zh", "x", "y", "zl", "c"), 0, 0)
    q0 = finish(q_finish_kernel, (q_own, back, cos, sin), (2, 128, 256), "q_finish")
    q1, q2 = to_rep(q0, 1), to_rep(q0, 2)
    qs = [q0, q1, q2, to_rep(q2, 1)]

    kept, sent = attend(idx, qs, pair_all.reshape(32, 4, 32, 128))
    (part,) = small(merge_kernel, (kept, to_rep(sent, 1)), [(ROWS, 256)], "merge")
    (mine,) = small(last_kernel, (part, to_rep(part, 2)), [(256, 512)], "last")
    (out,) = small(place_kernel, (idx, mine, to_rep(mine, 1)), [(256, 1024)], "place", 1)
    return out


def solution(mesh):
    grid = Mesh(mesh.devices.reshape(2, 2, 2, 4, 4), ("zl", "c", "zh", "x", "y"))
    fsdp = ("zh", "x", "y")
    in_specs = (P(fsdp, None), P(REP, fsdp, None), P(REP, fsdp, None), P())
    return jax.shard_map(
        local, mesh=grid, in_specs=in_specs, out_specs=P(fsdp, None), check_vma=False
    )
```
